32 devices in a mesh: gx: 8 (over y, x, core), gy: 4 (over z).
Axes of the slice: x: 2, y: 2, z: 4, core: 2. Of those that a mesh axis runs over, the one named last changes fastest.
Arguments:
- mass_per_volume: float32 [64, 32, 128], P('gx', 'gy'), may hold values from 0.4 to 2.5
- velocity: float32 [3, 64, 32, 128], P(None, 'gx', 'gy'), may hold values from -3 to 3
- thermal_stress: float32 [64, 32, 128], P('gx', 'gy'), may hold values from 0.06 to 1.5
- magnetic: float32 [3, 64, 32, 128], P(None, 'gx', 'gy'), may hold values from -4.8 to 4.8, as said below
Outputs:
- density_out: float32 [64, 32, 128], P('gx', 'gy')
- velocity_out: float32 [3, 64, 32, 128], P(None, 'gx', 'gy')
- pressure_out: float32 [64, 32, 128], P('gx', 'gy')
- magnetic_out: float32 [3, 64, 32, 128], P(None, 'gx', 'gy')
The draws below stay inside these ranges and needn't reach their ends.
Inputs may be any that keep to these rules, and one draw needn't show every extreme that they name: magnetic has zero discrete divergence in every cell: the sum over c of b_c at i+1 minus b_c at i along c vanishes up to rounding.
All inputs are finite; a program needn't handle non-finite values.
Results may differ from the reference program's by a relative error of at most 0.0003.
Values sent between devices are 32-bit elements; how exact they have to be, the bound alone decides.
A program may use at most 128 MiB of HBM per device.

```python
import math
import jax
import jax.numpy as jnp
from jax import lax

CX = 8
NZ = 128
SECTIONS = 4
SUPER_SECTIONS = 8
NX = 64
NY = 32


def draw_magnetic(key, part):
    potential = jnp.clip(0.35 * jax.random.normal(key, (3, NX, NY, NZ), jnp.float32), -1.2, 1.2)
    vector_x = potential[0]
    vector_y = potential[1]
    vector_z = potential[2]
    face_x = jnp.roll(vector_z, -1, 1) - vector_z - (jnp.roll(vector_y, -1, 2) - vector_y)
    face_y = jnp.roll(vector_x, -1, 2) - vector_x - (jnp.roll(vector_z, -1, 0) - vector_z)
    face_z = jnp.roll(vector_y, -1, 0) - vector_y - (jnp.roll(vector_x, -1, 1) - vector_x)
    return jnp.stack([face_x, face_y, face_z])


def shard_levels(own_key, shape, cuts, least, largest):
    loudness, own = 1.0, jax.random.fold_in(own_key, 6)
    for axis_at, blocks in cuts:
        heights = jnp.exp(jax.random.uniform(jax.random.fold_in(own, axis_at), (blocks,), jnp.float32, least / len(cuts), largest / len(cuts)))
        loudness = loudness * jnp.repeat(heights, shape[axis_at] // blocks).reshape([-1 if axis == axis_at else 1 for axis in range(len(shape))])
    return loudness


def normal_values(stream_key, shape, scale, reach, pieces=(), kind=jnp.bfloat16):
    entries = scale * jax.random.normal(stream_key, shape, jnp.float32)
    if pieces:
        entries = entries * shard_levels(stream_key, shape, pieces, -0.22, 0.18)
    return jnp.clip(entries, -reach, reach).astype(kind)


def setup_inputs(seed: int = 0) -> dict:
    streams_of = jax.random.split(jax.random.key(seed), 5)
    mass_per_volume = jnp.clip(jnp.exp(math.log(2.5) - 1.8325814 * jax.random.uniform(streams_of[0], (NX, NY, NZ), jnp.float32) ** shard_levels(streams_of[0], (NX, NY, NZ), ((0, 8), (1, 4)), -0.2, 0.2)), 0.4, 2.5)
    velocity = normal_values(streams_of[1], (3, NX, NY, NZ), 0.5, 3.0, ((1, 8), (2, 4)), jnp.float32)
    thermal_stress = jnp.clip(jnp.exp(math.log(1.5) - 3.218876 * jax.random.uniform(streams_of[2], (NX, NY, NZ), jnp.float32) ** shard_levels(streams_of[2], (NX, NY, NZ), ((0, 8), (1, 4)), -0.2, 0.2)), 0.06, 1.5)
    magnetic = draw_magnetic(jax.random.fold_in(streams_of[4], 71), 0)
    return {"mass_per_volume": mass_per_volume, "velocity": velocity, "thermal_stress": thermal_stress, "magnetic": magnetic}


GAMMA_RATIO = 5.0 / 3.0
TIME_STEP = 0.04
SUPER_TIME = 0.08
DENSITY_FLOOR = 0.5
PRESSURE_FLOOR = 0.1
FIELD_FLOOR = 0.05

def adjacent_zone(a, dimension, k):
    return jnp.roll(a, -k, dimension)

def minmod(lower, upper):
    return 0.5 * (jnp.sign(lower) + jnp.sign(upper)) * jnp.minimum(jnp.abs(lower), jnp.abs(upper))

def wave_fluxes(mass_per_volume, velocity, thermal_stress, magnetic, adjacent_quantities):
    magnetic_sq = magnetic[0] * magnetic[0] + magnetic[1] * magnetic[1] + magnetic[2] * magnetic[2]
    kinetic = velocity[0] * velocity[0] + velocity[1] * velocity[1] + velocity[2] * velocity[2]
    whole_work_content = thermal_stress / (GAMMA_RATIO - 1.0) + 0.5 * mass_per_volume * kinetic + 0.5 * magnetic_sq
    pressure_total = thermal_stress + 0.5 * magnetic_sq
    normal_speed = velocity[adjacent_quantities]
    normal_field = magnetic[adjacent_quantities]
    projection = velocity[0] * magnetic[0] + velocity[1] * magnetic[1] + velocity[2] * magnetic[2]
    others = [zone_quantities for zone_quantities in range(3) if zone_quantities != adjacent_quantities]
    conserved = [mass_per_volume] + [mass_per_volume * velocity[zone_quantities] for zone_quantities in range(3)] + [whole_work_content] + [magnetic[zone_quantities] for zone_quantities in others]
    momentum_fluxes = []
    for zone_quantities in range(3):
        momentum_term = mass_per_volume * normal_speed * velocity[zone_quantities] - normal_field * magnetic[zone_quantities]
        if zone_quantities == adjacent_quantities:
            momentum_term = momentum_term + pressure_total
        momentum_fluxes.append(momentum_term)
    fluxes = [mass_per_volume * normal_speed] + momentum_fluxes
    fluxes = fluxes + [(whole_work_content + pressure_total) * normal_speed - normal_field * projection]
    fluxes = fluxes + [normal_speed * magnetic[zone_quantities] - velocity[zone_quantities] * normal_field for zone_quantities in others]
    signal = jnp.abs(normal_speed) + jnp.sqrt((GAMMA_RATIO * thermal_stress + magnetic_sq) / mass_per_volume)
    return (conserved, fluxes, signal)

def face_fluxes(mass_per_volume, velocity, thermal_stress, cell_field, face_field, adjacent_quantities):
    primitive = [mass_per_volume] + list(velocity) + [thermal_stress] + list(cell_field)
    lower_states = []
    upper_states = []
    for n in range(8):
        if n == 5 + adjacent_quantities:
            lower_states.append(face_field[adjacent_quantities])
            upper_states.append(face_field[adjacent_quantities])
        else:
            quantity = primitive[n]
            gradient = minmod(quantity - adjacent_zone(quantity, adjacent_quantities, -1), adjacent_zone(quantity, adjacent_quantities, 1) - quantity)
            lower_states.append(adjacent_zone(quantity + 0.5 * gradient, adjacent_quantities, -1))
            upper_states.append(quantity - 0.5 * gradient)
    conserved_lower, flux_lower, signal_lower = wave_fluxes(lower_states[0], lower_states[1:4], lower_states[4], lower_states[5:8], adjacent_quantities)
    conserved_upper, flux_upper, signal_upper = wave_fluxes(upper_states[0], upper_states[1:4], upper_states[4], upper_states[5:8], adjacent_quantities)
    signal = jnp.maximum(signal_lower, signal_upper)
    return [0.5 * (flux_lower[n] + flux_upper[n]) - 0.5 * signal * (conserved_upper[n] - conserved_lower[n]) for n in range(7)]

def hyperbolic(mass_per_volume, velocity, thermal_stress, face_field):
    cell_field = [0.5 * (face_field[zone_quantities] + adjacent_zone(face_field[zone_quantities], zone_quantities, 1)) for zone_quantities in range(3)]
    momentum = [mass_per_volume * velocity[zone_quantities] for zone_quantities in range(3)]
    kinetic = velocity[0] * velocity[0] + velocity[1] * velocity[1] + velocity[2] * velocity[2]
    magnetic_sq = cell_field[0] * cell_field[0] + cell_field[1] * cell_field[1] + cell_field[2] * cell_field[2]
    whole_work_content = thermal_stress / (GAMMA_RATIO - 1.0) + 0.5 * mass_per_volume * kinetic + 0.5 * magnetic_sq
    conserved = [mass_per_volume] + momentum + [whole_work_content]
    directional = [face_fluxes(mass_per_volume, velocity, thermal_stress, cell_field, face_field, adjacent_quantities) for adjacent_quantities in range(3)]
    updated = []
    for n in range(5):
        change = conserved[n]
        for adjacent_quantities in range(3):
            change = change - TIME_STEP * (adjacent_zone(directional[adjacent_quantities][n], adjacent_quantities, 1) - directional[adjacent_quantities][n])
        updated.append(change)

    def induction(adjacent_quantities, zone_quantities):
        others = [e for e in range(3) if e != adjacent_quantities]
        return directional[adjacent_quantities][5 + others.index(zone_quantities)]
    x_flux_y = induction(0, 1)
    y_flux_x = induction(1, 0)
    x_flux_z = induction(0, 2)
    z_flux_x = induction(2, 0)
    y_flux_z = induction(1, 2)
    z_flux_y = induction(2, 1)
    edge_z = 0.25 * (adjacent_zone(y_flux_x, 0, -1) + y_flux_x - adjacent_zone(x_flux_y, 1, -1) - x_flux_y)
    edge_y = 0.25 * (adjacent_zone(x_flux_z, 2, -1) + x_flux_z - adjacent_zone(z_flux_x, 0, -1) - z_flux_x)
    edge_x = 0.25 * (adjacent_zone(z_flux_y, 1, -1) + z_flux_y - adjacent_zone(y_flux_z, 2, -1) - y_flux_z)
    new_face = [face_field[0] - TIME_STEP * (adjacent_zone(edge_z, 1, 1) - edge_z) + TIME_STEP * (adjacent_zone(edge_y, 2, 1) - edge_y), face_field[1] - TIME_STEP * (adjacent_zone(edge_x, 2, 1) - edge_x) + TIME_STEP * (adjacent_zone(edge_z, 0, 1) - edge_z), face_field[2] - TIME_STEP * (adjacent_zone(edge_y, 0, 1) - edge_y) + TIME_STEP * (adjacent_zone(edge_x, 1, 1) - edge_x)]
    floored = jnp.maximum(updated[0], DENSITY_FLOOR)
    new_velocity = [updated[1 + zone_quantities] / floored for zone_quantities in range(3)]
    new_cell = [0.5 * (new_face[zone_quantities] + adjacent_zone(new_face[zone_quantities], zone_quantities, 1)) for zone_quantities in range(3)]
    kinetic_new = updated[1] * new_velocity[0] + updated[2] * new_velocity[1] + updated[3] * new_velocity[2]
    magnetic_new = new_cell[0] * new_cell[0] + new_cell[1] * new_cell[1] + new_cell[2] * new_cell[2]
    internal = updated[4] - 0.5 * kinetic_new - 0.5 * magnetic_new
    new_pressure = jnp.maximum((GAMMA_RATIO - 1.0) * internal, PRESSURE_FLOOR)
    return (floored, new_velocity, new_pressure, new_face)

def coefficients(mass_per_volume, thermal_stress, face_field):
    plasma_thermal_level = thermal_stress / mass_per_volume
    thermal_diffusion_coefficient = plasma_thermal_level * plasma_thermal_level * jnp.sqrt(plasma_thermal_level)
    cell_field = [0.5 * (face_field[zone_quantities] + adjacent_zone(face_field[zone_quantities], zone_quantities, 1)) for zone_quantities in range(3)]
    coupling = []
    for adjacent_quantities in range(3):
        components = []
        for zone_quantities in range(3):
            if zone_quantities == adjacent_quantities:
                components.append(face_field[adjacent_quantities])
            else:
                components.append(0.5 * (cell_field[zone_quantities] + adjacent_zone(cell_field[zone_quantities], adjacent_quantities, -1)))
        magnitude = components[0] * components[0] + components[1] * components[1] + components[2] * components[2]
        factor = 0.5 * (thermal_diffusion_coefficient + adjacent_zone(thermal_diffusion_coefficient, adjacent_quantities, -1)) / jnp.maximum(magnitude, FIELD_FLOOR)
        coupling.append([factor * face_field[adjacent_quantities] * components[zone_quantities] for zone_quantities in range(3)])
    return coupling

def conduction(whole_work_content, mass_per_volume, coupling):
    plasma_thermal_level = (GAMMA_RATIO - 1.0) * whole_work_content / mass_per_volume
    middle_derivative = [0.5 * (adjacent_zone(plasma_thermal_level, zone_quantities, 1) - adjacent_zone(plasma_thermal_level, zone_quantities, -1)) for zone_quantities in range(3)]
    result = jnp.zeros_like(whole_work_content)
    for adjacent_quantities in range(3):
        clipped_derivatives = []
        for zone_quantities in range(3):
            if zone_quantities == adjacent_quantities:
                clipped_derivatives.append(plasma_thermal_level - adjacent_zone(plasma_thermal_level, adjacent_quantities, -1))
            else:
                clipped_derivatives.append(0.5 * (middle_derivative[zone_quantities] + adjacent_zone(middle_derivative[zone_quantities], adjacent_quantities, -1)))
        heat_flux = -(coupling[adjacent_quantities][0] * clipped_derivatives[0] + coupling[adjacent_quantities][1] * clipped_derivatives[1] + coupling[adjacent_quantities][2] * clipped_derivatives[2])
        result = result - (adjacent_zone(heat_flux, adjacent_quantities, 1) - heat_flux)
    return result

def super_step(whole_work_content, initial_rate, operator):
    b = [1.0 / 3.0, 1.0 / 3.0, 1.0 / 3.0] + [(j * j + j - 2.0) / (2.0 * j * (j + 1.0)) for j in range(3, SUPER_SECTIONS + 1)]
    base_rate = 4.0 / (SUPER_SECTIONS * SUPER_SECTIONS + SUPER_SECTIONS - 2.0)
    earlier = whole_work_content
    latest = whole_work_content + b[1] * base_rate * SUPER_TIME * initial_rate
    for j in range(2, SECTIONS + 1):
        factor_prev = (2.0 * j - 1.0) / j * b[j] / b[j - 1]
        factor_back = -(j - 1.0) / j * b[j] / b[j - 2]
        factor_rate = factor_prev * base_rate
        factor_zero = -(1.0 - b[j - 1]) * factor_rate
        advanced = factor_prev * latest + factor_back * earlier + (1.0 - factor_prev - factor_back) * whole_work_content + factor_rate * SUPER_TIME * operator(latest) + factor_zero * SUPER_TIME * initial_rate
        earlier = latest
        latest = advanced
    return latest

def advance(stacked):
    mass_per_volume, velocity, thermal_stress, face_field = hyperbolic(stacked[0], [stacked[1], stacked[2], stacked[3]], stacked[4], [stacked[5], stacked[6], stacked[7]])
    coupling = coefficients(mass_per_volume, thermal_stress, face_field)
    whole_work_content = thermal_stress / (GAMMA_RATIO - 1.0)
    initial_rate = conduction(whole_work_content, mass_per_volume, coupling)
    closing = super_step(whole_work_content, initial_rate, lambda e: conduction(e, mass_per_volume, coupling))
    return jnp.stack([mass_per_volume] + velocity + [(GAMMA_RATIO - 1.0) * closing] + face_field)

def reference(mass_per_volume, velocity, thermal_stress, magnetic):
    stacked = jnp.concatenate([mass_per_volume[None], velocity, thermal_stress[None], magnetic], axis=0)
    margin = 3 + SECTIONS

    def one_slab(offset):
        row_index = (jnp.arange(CX + 2 * margin, dtype=jnp.int32) + offset - margin) % NX
        window_state = jnp.take(stacked, row_index.astype(jnp.int32), axis=1)
        return advance(window_state)[:, margin:margin + CX]
    starts = jnp.arange(NX // CX, dtype=jnp.int32) * CX
    blocks = lax.map(one_slab, starts)
    result = jnp.moveaxis(blocks, 0, 1).reshape(8, NX, NY, NZ)
    return (result[0], result[1:4], result[4], result[5:8])
```

```python
import functools

import jax
import jax.numpy as jnp
from jax import lax
from jax.experimental import pallas as pl
from jax.experimental.pallas import tpu as pltpu
from jax.sharding import PartitionSpec as P

SECTIONS = 4
SUPER_SECTIONS = 8

G = 5.0 / 3.0
DT = 0.04
SUPER_TIME = 0.08
DENSITY_FLOOR = 0.5
PRESSURE_FLOOR = 0.1
FIELD_FLOOR = 0.05

MESH = pl.DeviceIdType.MESH

H = 3
ROWS = 16


def ylow(a):
    return pltpu.roll(a, 1, 0)


def yhigh(a):
    return pltpu.roll(a, a.shape[0] - 1, 0)


def zlow(a):
    return pltpu.roll(a, 1, 1)


def zhigh(a):
    return pltpu.roll(a, a.shape[1] - 1, 1)


def minmod(a, b):
    return jnp.maximum(jnp.minimum(a, b), 0.0) + jnp.minimum(jnp.maximum(a, b), 0.0)


def wave(rho, v, p, b, d):
    bsq = b[0] * b[0] + b[1] * b[1] + b[2] * b[2]
    ksq = v[0] * v[0] + v[1] * v[1] + v[2] * v[2]
    half = 0.5 * bsq
    energy = p * 1.5 + 0.5 * rho * ksq + half
    total = p + half
    vn, bn = v[d], b[d]
    proj = v[0] * b[0] + v[1] * b[1] + v[2] * b[2]
    others = [c for c in range(3) if c != d]
    m = [rho * v[c] for c in range(3)]
    cons = [rho] + m + [energy] + [b[c] for c in others]
    mom = []
    for c in range(3):
        t = m[d] * v[c] - bn * b[c]
        mom.append(t + total if c == d else t)
    flux = [m[d]] + mom + [(energy + total) * vn - bn * proj]
    flux += [vn * b[c] - v[c] * bn for c in others]
    a = G * p + bsq
    signal = jnp.abs(vn) + a * lax.rsqrt(a * rho)
    return cons, flux, signal


def face_flux(lower, upper, bn, d):
    def split(s):
        rest = list(s[5:])
        rest.insert(d, bn)
        return s[0], s[1:4], s[4], rest

    ul, fl, sl = wave(*split(lower), d)
    uu, fu, su = wave(*split(upper), d)
    signal = jnp.maximum(sl, su)
    return [0.5 * ((fl[n] + fu[n]) - signal * (uu[n] - ul[n])) for n in range(7)]


def along(prims, bn, d):
    low, high = (ylow, yhigh) if d == 1 else (zlow, zhigh)
    lower, upper = [], []
    for q in prims:
        diff = q - low(q)
        half = 0.5 * minmod(diff, high(diff))
        lower.append(low(q + half))
        upper.append(q - half)
    return face_flux(lower, upper, bn, d)


def rkl_factors():
    b = [1.0 / 3.0] * 3 + [
        (j * j + j - 2.0) / (2.0 * j * (j + 1.0)) for j in range(3, SUPER_SECTIONS + 1)
    ]
    w = 4.0 / (SUPER_SECTIONS * SUPER_SECTIONS + SUPER_SECTIONS - 2.0)
    rows = []
    for j in range(2, SECTIONS + 1):
        mu = (2.0 * j - 1.0) / j * b[j] / b[j - 1]
        nu = -(j - 1.0) / j * b[j] / b[j - 2]
        rate = mu * w * SUPER_TIME
        rows.append((mu, nu, 1.0 - mu - nu, rate, -(1.0 - b[j - 1]) * rate))
    return b[1] * w * SUPER_TIME, rows


def kernel(
    nx, ny,
    rho_ref, v_ref, p_ref, b_ref,
    o_rho, o_v, o_p, o_b,
    ext, up, down, from_low, from_high,
    lower_s, diff_s, cell_s, d_s, f_s, b_s,
    irho_s, e_s, kap_s, bc_s, bf_s, kx_s, ky_s, kz_s,
    t_s, pk, low_row, high_row,
    send_sem, recv_sem,
):
    cx = rho_ref.shape[0]
    cy = rho_ref.shape[1]
    gx, gy = lax.axis_index("gx"), lax.axis_index("gy")

    def target(dx, dy):
        return (lax.rem(gx + dx + nx, nx), lax.rem(gy + dy + ny, ny))

    ring = [(dx, dy) for dy in (1, -1, 0) for dx in (0, 1, -1) if (dx, dy) != (0, 0)]

    barrier = pltpu.get_barrier_semaphore()
    for dx, dy in ring:
        pl.semaphore_signal(barrier, inc=1, device_id=target(dx, dy), device_id_type=MESH)

    fields = [rho_ref] + [v_ref.at[c] for c in range(3)] + [p_ref] + [b_ref.at[c] for c in range(3)]
    for f, ref in enumerate(fields):
        value = ref[...]
        up[:, H * f : H * f + H, :] = value[:, cy - H : cy, :]
        down[:, H * f : H * f + H, :] = value[:, 0:H, :]
        ext[f, H : H + cx, 0:cy, :] = value
    pl.semaphore_wait(barrier, len(ring))

    def remote(phase, k, src, dst):
        copy = pltpu.make_async_remote_copy(
            src_ref=src,
            dst_ref=dst,
            send_sem=send_sem.at[phase, k],
            recv_sem=recv_sem.at[phase, k],
            device_id=target(*ring[k]),
            device_id_type=MESH,
        )
        copy.start()
        return copy

    copies = []
    for k, (dx, dy) in enumerate(ring):
        if dx == 0:
            here, there = slice(0, cx), slice(H, H + cx)
        elif dx == 1:
            here, there = slice(cx - H, cx), slice(0, H)
        else:
            here, there = slice(0, H), slice(H + cx, 2 * H + cx)
        here = pl.ds(here.start, here.stop - here.start)
        there = pl.ds(there.start, there.stop - there.start)
        if dy == 1:
            copies.append(remote(0, k, up.at[here], from_low.at[there]))
        elif dy == -1:
            copies.append(remote(0, k, down.at[here], from_high.at[there]))
        else:
            src = pl.ds(here.start + H, here.size)
            copies.append(
                remote(0, k, ext.at[:, src, pl.ds(0, cy)], ext.at[:, there, pl.ds(0, cy)])
            )

    one = jnp.ones((ROWS, 128), jnp.float32)
    for ref in (lower_s, diff_s, cell_s, d_s, f_s, b_s):
        for n in range(ref.shape[0]):
            ref[n] = one
    for copy in copies:
        copy.wait()

    def unpack(s, carry):
        for f in range(8):
            ext[f, s, cy:ROWS, :] = jnp.ones((ROWS - cy, 128), jnp.float32)
            ext[f, s, cy : cy + H, :] = from_high[s, H * f : H * f + H, :]
            ext[f, s, ROWS - H : ROWS, :] = from_low[s, H * f : H * f + H, :]
        return carry

    lax.fori_loop(0, cx + 2 * H, unpack, 0)

    def cells(s):
        by, bz = ext[6, s], ext[7, s]
        return [0.5 * (by + yhigh(by)), 0.5 * (bz + zhigh(bz))]

    def raw(s):
        return [ext[f, s] for f in range(5)] + cells(s)

    first, second = raw(0), raw(1)
    for n in range(7):
        diff_s[n] = second[n] - first[n]
    cell_s[0] = second[5]
    cell_s[1] = second[6]

    def body(i, carry):
        here = [ext[f, i] for f in range(5)] + [cell_s[0], cell_s[1]]
        there = raw(i + 1)
        bx, by, bz = ext[5, i], ext[6, i], ext[7, i]
        cell = [0.5 * (bx + ext[5, i + 1]), here[5], here[6]]
        lower = [lower_s[n] for n in range(7)]
        upper = []
        for n in range(7):
            diff = there[n] - here[n]
            half = 0.5 * minmod(diff_s[n], diff)
            diff_s[n] = diff
            upper.append(here[n] - half)
            lower_s[n] = here[n] + half
        cell_s[0] = there[5]
        cell_s[1] = there[6]
        fx = face_flux(lower, upper, bx, 0)
        fy = along(here[:5] + [cell[0], cell[2]], by, 1)
        fz = along(here[:5] + [cell[0], cell[1]], bz, 2)

        ez = 0.25 * (f_s[0] + fy[5] - ylow(fx[5]) - fx[5])
        ey = 0.25 * (zlow(fx[6]) + fx[6] - f_s[1] - fz[5])
        ex = 0.25 * (ylow(fz[6]) + fz[6] - zlow(fy[6]) - fy[6])
        f_s[0] = fy[5]
        f_s[1] = fz[5]
        bxn = bx - DT * (yhigh(ez) - ez) + DT * (zhigh(ey) - ey)
        bxo = b_s[0]
        byn = b_s[1] + DT * ez
        bzn = b_s[2] - DT * ey
        b_s[0] = bxn
        b_s[1] = by - DT * (zhigh(ex) - ex) - DT * ez
        b_s[2] = bz + DT * ey + DT * (yhigh(ex) - ex)

        rho, v, p = here[0], here[1:4], here[4]
        energy = (
            p * 1.5
            + 0.5 * rho * (v[0] * v[0] + v[1] * v[1] + v[2] * v[2])
            + 0.5 * (cell[0] * cell[0] + cell[1] * cell[1] + cell[2] * cell[2])
        )
        cons = [rho, rho * v[0], rho * v[1], rho * v[2], energy]
        new = [d_s[n] - DT * fx[n] for n in range(5)]
        for n in range(5):
            d_s[n] = cons[n] - DT * ((yhigh(fy[n]) - fy[n]) + (zhigh(fz[n]) - fz[n]) - fx[n])

        m = i - 1
        floored = jnp.maximum(new[0], DENSITY_FLOOR)
        inv = 1.0 / floored
        vel = [new[1 + c] * inv for c in range(3)]
        bc = [0.5 * (bxo + bxn), 0.5 * (byn + yhigh(byn)), 0.5 * (bzn + zhigh(bzn))]
        kinetic = new[1] * vel[0] + new[2] * vel[1] + new[3] * vel[2]
        internal = new[4] - 0.5 * kinetic - 0.5 * (bc[0] * bc[0] + bc[1] * bc[1] + bc[2] * bc[2])
        p1 = jnp.maximum((G - 1.0) * internal, PRESSURE_FLOOR)
        t = p1 * inv
        irho_s[m] = (G - 1.0) * inv
        e_s[m] = p1 * 1.5
        t_s[0, m] = t
        kap_s[m] = t * t * jnp.sqrt(t)
        for c in range(3):
            bc_s[c, m] = bc[c]
        for c, a in enumerate((bxo, byn, bzn)):
            bf_s[c, m] = a

        @pl.when(jnp.logical_and(m >= H, m < H + cx))
        def _():
            x = jnp.clip(m - H, 0, cx - 1)
            o_rho[x] = floored[0:cy]
            for c in range(3):
                o_v[c, x] = vel[c][0:cy]
            for c, a in enumerate((bxo, byn, bzn)):
                o_b[c, x] = a[0:cy]

        return carry

    lax.fori_loop(1, cx + 2 * H - 1, body, 0)

    def coupling(s, carry):
        kap = kap_s[s]
        bc = [bc_s[c, s] for c in range(3)]
        bf = [bf_s[c, s] for c in range(3)]
        for d, out in enumerate((kx_s, ky_s, kz_s)):
            if d == 0:
                kl, bl = kap_s[s - 1], [bc_s[c, s - 1] for c in range(3)]
            else:
                low = ylow if d == 1 else zlow
                kl, bl = low(kap), [low(bc[c]) if c != d else None for c in range(3)]
            comp = [bf[d] if c == d else 0.5 * (bc[c] + bl[c]) for c in range(3)]
            mag = comp[0] * comp[0] + comp[1] * comp[1] + comp[2] * comp[2]
            factor = 0.5 * (kap + kl) / jnp.maximum(mag, FIELD_FLOOR) * bf[d]
            rows = ROWS if d == 1 else cy
            for c in range(3):
                k = factor * comp[c] * (1.0 if c == d else 0.25)
                out[c, s - H] = k[0:rows]
        return carry

    lax.fori_loop(H, H + cx + 1, coupling, 0)

    def rate(phase):
        t = [t_s[phase, H - 1 + s] for s in range(cx + 2)]
        ts = [a[0:cy] for a in t]
        dz = [zhigh(a) - zlow(a) for a in t]
        dy = [(yhigh(a) - ylow(a))[0:cy] for a in t]
        out = []
        qx = []
        for x in range(cx + 1):
            qx.append(
                kx_s[0, x] * (ts[x + 1] - ts[x])
                + kx_s[1, x] * (dy[x] + dy[x + 1])
                + kx_s[2, x] * (dz[x] + dz[x + 1])[0:cy]
            )
        for x in range(cx):
            a = t[x + 1]
            dx = t[x + 2] - t[x]
            qy = (
                ky_s[1, x] * (a - ylow(a))
                + ky_s[0, x] * (dx + ylow(dx))
                + ky_s[2, x] * (dz[x + 1] + ylow(dz[x + 1]))
            )
            dxs = dx[0:cy]
            qz = (
                kz_s[2, x] * (ts[x + 1] - zlow(ts[x + 1]))
                + kz_s[0, x] * (dxs + zlow(dxs))
                + kz_s[1, x] * (dy[x + 1] + zlow(dy[x + 1]))
            )
            out.append(qx[x + 1] - qx[x] + (yhigh(qy) - qy)[0:cy] + (zhigh(qz) - qz))
        return jnp.stack(out)

    first_factor, factors = rkl_factors()
    inner = pl.ds(H, cx)
    base = e_s[inner, 0:cy, :]
    irho = irho_s[inner, 0:cy, :]
    rate0 = rate(0)
    earlier, latest = base, base + first_factor * rate0
    for n, (mu, nu, rest, fresh, zero) in enumerate(factors):
        phase = n + 1
        t = latest * irho
        for x in range(cx):
            pk[n, 0, x : x + 1, :] = t[x, cy - 1 : cy, :]
            pk[n, 1, x : x + 1, :] = t[x, 0:1, :]
        t_s[phase, inner, 0:cy, :] = t
        copies = []
        for k, (dx, dy) in enumerate(ring):
            if dy == 1:
                copies.append(remote(phase, k, pk.at[n, 0], low_row.at[n, dx + 1]))
            elif dy == -1:
                copies.append(remote(phase, k, pk.at[n, 1], high_row.at[n, dx + 1]))
            else:
                src = H + cx - 1 if dx == 1 else H
                dst = H - 1 if dx == 1 else H + cx
                copies.append(
                    remote(
                        phase, k,
                        t_s.at[phase, src, pl.ds(0, cy)],
                        t_s.at[phase, dst, pl.ds(0, cy)],
                    )
                )
        part = mu * latest + nu * earlier + rest * base + zero * rate0
        for copy in copies:
            copy.wait()
        for s in range(cx + 2):
            if s == 0:
                d, x = 2, cx - 1
            elif s == cx + 1:
                d, x = 0, 0
            else:
                d, x = 1, s - 1
            t_s[phase, H - 1 + s, cy : cy + 1, :] = high_row[n, d, x : x + 1, :]
            t_s[phase, H - 1 + s, ROWS - 1 : ROWS, :] = low_row[n, d, x : x + 1, :]
        earlier, latest = latest, part + fresh * rate(phase)
    o_p[...] = (G - 1.0) * latest


def solution(mesh):
    nx, ny = mesh.shape["gx"], mesh.shape["gy"]

    def local(rho, v, p, b):
        cx, cy, nz = rho.shape
        wide = cx + 2 * H
        f32 = jnp.float32
        vm = lambda *shape: pltpu.VMEM(shape, f32)
        phases = SECTIONS - 1
        spec = pl.BlockSpec(memory_space=pltpu.VMEM)
        return pl.pallas_call(
            functools.partial(kernel, nx, ny),
            out_shape=[
                jax.ShapeDtypeStruct(rho.shape, f32),
                jax.ShapeDtypeStruct(v.shape, f32),
                jax.ShapeDtypeStruct(p.shape, f32),
                jax.ShapeDtypeStruct(b.shape, f32),
            ],
            in_specs=[spec] * 4,
            out_specs=[spec] * 4,
            scratch_shapes=[
                vm(8, wide, ROWS, nz),
                vm(cx, 8 * H, nz),
                vm(cx, 8 * H, nz),
                vm(wide, 8 * H, nz),
                vm(wide, 8 * H, nz),
                vm(7, ROWS, nz),
                vm(7, ROWS, nz),
                vm(2, ROWS, nz),
                vm(5, ROWS, nz),
                vm(2, ROWS, nz),
                vm(3, ROWS, nz),
                vm(wide, ROWS, nz),
                vm(wide, ROWS, nz),
                vm(wide, ROWS, nz),
                vm(3, wide, ROWS, nz),
                vm(3, wide, ROWS, nz),
                vm(3, cx + 1, cy, nz),
                vm(3, cx + 1, ROWS, nz),
                vm(3, cx + 1, cy, nz),
                vm(SECTIONS, wide, ROWS, nz),
                vm(phases, 2, cx, nz),
                vm(phases, 3, cx, nz),
                vm(phases, 3, cx, nz),
                pltpu.SemaphoreType.DMA((SECTIONS, 8)),
                pltpu.SemaphoreType.DMA((SECTIONS, 8)),
            ],
            compiler_params=pltpu.CompilerParams(collective_id=0, has_side_effects=True),
        )(rho, v, p, b)

    placed = (
        P("gx", "gy", None),
        P(None, "gx", "gy", None),
        P("gx", "gy", None),
        P(None, "gx", "gy", None),
    )
    return jax.shard_map(
        lambda *a: tuple(local(*a)),
        mesh=mesh,
        in_specs=placed,
        out_specs=placed,
        check_vma=False,
    )
```

```python
import functools

import jax
import jax.numpy as jnp
from jax import lax
from jax.experimental import pallas as pl
from jax.experimental.pallas import tpu as pltpu
from jax.sharding import PartitionSpec as P

SECTIONS = 4
SUPER_SECTIONS = 8

G = 5.0 / 3.0
DT = 0.04
SUPER_TIME = 0.08
DENSITY_FLOOR = 0.5
PRESSURE_FLOOR = 0.1
FIELD_FLOOR = 0.05

MESH = pl.DeviceIdType.MESH

H = 3
ROWS = 16


def ylow(a):
    return pltpu.roll(a, 1, 0)


def yhigh(a):
    return pltpu.roll(a, a.shape[0] - 1, 0)


def zlow(a):
    return pltpu.roll(a, 1, 1)


def zhigh(a):
    return pltpu.roll(a, a.shape[1] - 1, 1)


def minmod(a, b):
    return jnp.maximum(jnp.minimum(a, b), 0.0) + jnp.minimum(jnp.maximum(a, b), 0.0)


def wave(rho, v, p, b, d):
    bsq = b[0] * b[0] + b[1] * b[1] + b[2] * b[2]
    ksq = v[0] * v[0] + v[1] * v[1] + v[2] * v[2]
    half = 0.5 * bsq
    energy = p * 1.5 + 0.5 * rho * ksq + half
    total = p + half
    vn, bn = v[d], b[d]
    proj = v[0] * b[0] + v[1] * b[1] + v[2] * b[2]
    others = [c for c in range(3) if c != d]
    m = [rho * v[c] for c in range(3)]
    cons = [rho] + m + [energy] + [b[c] for c in others]
    mom = []
    for c in range(3):
        t = m[d] * v[c] - bn * b[c]
        mom.append(t + total if c == d else t)
    flux = [m[d]] + mom + [(energy + total) * vn - bn * proj]
    flux += [vn * b[c] - v[c] * bn for c in others]
    a = G * p + bsq
    signal = jnp.abs(vn) + a * lax.rsqrt(a * rho)
    return cons, flux, signal


def face_flux(lower, upper, bn, d):
    def split(s):
        rest = list(s[5:])
        rest.insert(d, bn)
        return s[0], s[1:4], s[4], rest

    ul, fl, sl = wave(*split(lower), d)
    uu, fu, su = wave(*split(upper), d)
    signal = jnp.maximum(sl, su)
    return [0.5 * ((fl[n] + fu[n]) - signal * (uu[n] - ul[n])) for n in range(7)]


def along(prims, bn, d):
    low, high = (ylow, yhigh) if d == 1 else (zlow, zhigh)
    lower, upper = [], []
    for q in prims:
        diff = q - low(q)
        half = 0.5 * minmod(diff, high(diff))
        lower.append(low(q + half))
        upper.append(q - half)
    return face_flux(lower, upper, bn, d)


def rkl_factors():
    b = [1.0 / 3.0] * 3 + [
        (j * j + j - 2.0) / (2.0 * j * (j + 1.0)) for j in range(3, SUPER_SECTIONS + 1)
    ]
    w = 4.0 / (SUPER_SECTIONS * SUPER_SECTIONS + SUPER_SECTIONS - 2.0)
    rows = []
    for j in range(2, SECTIONS + 1):
        mu = (2.0 * j - 1.0) / j * b[j] / b[j - 1]
        nu = -(j - 1.0) / j * b[j] / b[j - 2]
        rate = mu * w * SUPER_TIME
        rows.append((mu, nu, 1.0 - mu - nu, rate, -(1.0 - b[j - 1]) * rate))
    return b[1] * w * SUPER_TIME, rows


def kernel(
    nx, ny,
    rho_ref, v_ref, p_ref, b_ref,
    rho_out, v_out, p_out, b_out,
    o_rho, o_v, o_p, o_b,
    ext, up, down, from_low, from_high,
    lower_s, diff_s, cell_s, d_s, f_s, b_s,
    irho_s, e_s, kap_s, bc_s, bf_s, kx_s, ky_s, kz_s,
    t_s, pk, low_row, high_row,
    send_sem, recv_sem, in_sem, out_sem,
):
    cx, cy = o_rho.shape[0], o_rho.shape[1]
    gx, gy = lax.axis_index("gx"), lax.axis_index("gy")

    def target(dx, dy):
        return (lax.rem(gx + dx + nx, nx), lax.rem(gy + dy + ny, ny))

    ring = [(dx, dy) for dy in (1, -1, 0) for dx in (0, 1, -1) if (dx, dy) != (0, 0)]

    barrier = pltpu.get_barrier_semaphore()
    for dx, dy in ring:
        pl.semaphore_signal(barrier, inc=1, device_id=target(dx, dy), device_id_type=MESH)

    own, near = pl.ds(H, cx), pl.ds(0, cy)
    places = [
        (rho_ref, ext.at[0, own, near]),
        (v_ref, ext.at[pl.ds(1, 3), own, near]),
        (p_ref, ext.at[4, own, near]),
        (b_ref, ext.at[pl.ds(5, 3), own, near]),
    ]
    loads = [
        pltpu.make_async_copy(src, dst, in_sem.at[n]) for n, (src, dst) in enumerate(places)
    ]
    for load in loads:
        load.start()
    for load in loads:
        load.wait()
    for f in range(8):
        value = ext[f, H : H + cx, 0:cy, :]
        up[:, H * f : H * f + H, :] = value[:, cy - H : cy, :]
        down[:, H * f : H * f + H, :] = value[:, 0:H, :]
    pl.semaphore_wait(barrier, len(ring))

    def remote(phase, k, src, dst):
        copy = pltpu.make_async_remote_copy(
            src_ref=src,
            dst_ref=dst,
            send_sem=send_sem.at[phase, k],
            recv_sem=recv_sem.at[phase, k],
            device_id=target(*ring[k]),
            device_id_type=MESH,
        )
        copy.start()
        return copy

    copies = []
    for k, (dx, dy) in enumerate(ring):
        if dx == 0:
            here, there = slice(0, cx), slice(H, H + cx)
        elif dx == 1:
            here, there = slice(cx - H, cx), slice(0, H)
        else:
            here, there = slice(0, H), slice(H + cx, 2 * H + cx)
        here = pl.ds(here.start, here.stop - here.start)
        there = pl.ds(there.start, there.stop - there.start)
        if dy == 1:
            copies.append(remote(0, k, up.at[here], from_low.at[there]))
        elif dy == -1:
            copies.append(remote(0, k, down.at[here], from_high.at[there]))
        else:
            src = pl.ds(here.start + H, here.size)
            copies.append(
                remote(0, k, ext.at[:, src, pl.ds(0, cy)], ext.at[:, there, pl.ds(0, cy)])
            )

    one = jnp.ones((ROWS, 128), jnp.float32)
    for ref in (lower_s, diff_s, cell_s, d_s, f_s, b_s):
        for n in range(ref.shape[0]):
            ref[n] = one
    for f in range(8):
        ext[f, :, cy:ROWS, :] = jnp.ones((cx + 2 * H, ROWS - cy, 128), jnp.float32)
    sent = list(copies)
    for copy in copies:
        copy.wait_recv()

    def unpack(s, carry):
        for f in range(8):
            ext[f, s, cy : cy + H, :] = from_high[s, H * f : H * f + H, :]
            ext[f, s, ROWS - H : ROWS, :] = from_low[s, H * f : H * f + H, :]
        return carry

    lax.fori_loop(0, cx + 2 * H, unpack, 0)

    def cells(s):
        by, bz = ext[6, s], ext[7, s]
        return [0.5 * (by + yhigh(by)), 0.5 * (bz + zhigh(bz))]

    def raw(s):
        return [ext[f, s] for f in range(5)] + cells(s)

    first, second = raw(0), raw(1)
    for n in range(7):
        diff_s[n] = second[n] - first[n]
    cell_s[0] = second[5]
    cell_s[1] = second[6]

    def body(i, carry):
        here = [ext[f, i] for f in range(5)] + [cell_s[0], cell_s[1]]
        there = raw(i + 1)
        bx, by, bz = ext[5, i], ext[6, i], ext[7, i]
        cell = [0.5 * (bx + ext[5, i + 1]), here[5], here[6]]
        lower = [lower_s[n] for n in range(7)]
        upper = []
        for n in range(7):
            diff = there[n] - here[n]
            half = 0.5 * minmod(diff_s[n], diff)
            diff_s[n] = diff
            upper.append(here[n] - half)
            lower_s[n] = here[n] + half
        cell_s[0] = there[5]
        cell_s[1] = there[6]
        fx = face_flux(lower, upper, bx, 0)
        fy = along(here[:5] + [cell[0], cell[2]], by, 1)
        fz = along(here[:5] + [cell[0], cell[1]], bz, 2)

        ez = 0.25 * (f_s[0] + fy[5] - ylow(fx[5]) - fx[5])
        ey = 0.25 * (zlow(fx[6]) + fx[6] - f_s[1] - fz[5])
        ex = 0.25 * (ylow(fz[6]) + fz[6] - zlow(fy[6]) - fy[6])
        f_s[0] = fy[5]
        f_s[1] = fz[5]
        bxn = bx - DT * (yhigh(ez) - ez) + DT * (zhigh(ey) - ey)
        bxo = b_s[0]
        byn = b_s[1] + DT * ez
        bzn = b_s[2] - DT * ey
        b_s[0] = bxn
        b_s[1] = by - DT * (zhigh(ex) - ex) - DT * ez
        b_s[2] = bz + DT * ey + DT * (yhigh(ex) - ex)

        rho, v, p = here[0], here[1:4], here[4]
        energy = (
            p * 1.5
            + 0.5 * rho * (v[0] * v[0] + v[1] * v[1] + v[2] * v[2])
            + 0.5 * (cell[0] * cell[0] + cell[1] * cell[1] + cell[2] * cell[2])
        )
        cons = [rho, rho * v[0], rho * v[1], rho * v[2], energy]
        new = [d_s[n] - DT * fx[n] for n in range(5)]
        for n in range(5):
            d_s[n] = cons[n] - DT * ((yhigh(fy[n]) - fy[n]) + (zhigh(fz[n]) - fz[n]) - fx[n])

        m = i - 1
        floored = jnp.maximum(new[0], DENSITY_FLOOR)
        inv = 1.0 / floored
        vel = [new[1 + c] * inv for c in range(3)]
        bc = [0.5 * (bxo + bxn), 0.5 * (byn + yhigh(byn)), 0.5 * (bzn + zhigh(bzn))]
        kinetic = new[1] * vel[0] + new[2] * vel[1] + new[3] * vel[2]
        internal = new[4] - 0.5 * kinetic - 0.5 * (bc[0] * bc[0] + bc[1] * bc[1] + bc[2] * bc[2])
        p1 = jnp.maximum((G - 1.0) * internal, PRESSURE_FLOOR)
        t = p1 * inv
        irho_s[m] = (G - 1.0) * inv
        e_s[m] = p1 * 1.5
        t_s[0, m] = t
        kap_s[m] = t * t * jnp.sqrt(t)
        for c in range(3):
            bc_s[c, m] = bc[c]
        for c, a in enumerate((bxo, byn, bzn)):
            bf_s[c, m] = a

        @pl.when(jnp.logical_and(m >= H, m < H + cx))
        def _():
            x = jnp.clip(m - H, 0, cx - 1)
            o_rho[x] = floored[0:cy]
            for c in range(3):
                o_v[c, x] = vel[c][0:cy]
            for c, a in enumerate((bxo, byn, bzn)):
                o_b[c, x] = a[0:cy]

        return carry

    lax.fori_loop(1, cx + 2 * H - 1, body, 0, unroll=2)
    stores = [
        pltpu.make_async_copy(src, dst, out_sem.at[n])
        for n, (src, dst) in enumerate(((o_rho, rho_out), (o_v, v_out), (o_b, b_out)))
    ]
    for store in stores:
        store.start()

    def coupling(s, carry):
        kap = kap_s[s]
        bc = [bc_s[c, s] for c in range(3)]
        bf = [bf_s[c, s] for c in range(3)]
        for d, out in enumerate((kx_s, ky_s, kz_s)):
            if d == 0:
                kl, bl = kap_s[s - 1], [bc_s[c, s - 1] for c in range(3)]
            else:
                low = ylow if d == 1 else zlow
                kl, bl = low(kap), [low(bc[c]) if c != d else None for c in range(3)]
            comp = [bf[d] if c == d else 0.5 * (bc[c] + bl[c]) for c in range(3)]
            mag = comp[0] * comp[0] + comp[1] * comp[1] + comp[2] * comp[2]
            factor = 0.5 * (kap + kl) / jnp.maximum(mag, FIELD_FLOOR) * bf[d]
            rows = ROWS if d == 1 else cy
            for c in range(3):
                k = factor * comp[c] * (1.0 if c == d else 0.25)
                out[c, s - H] = k[0:rows]
        return carry

    lax.fori_loop(H, H + cx + 1, coupling, 0)

    def rate(phase):
        t = [t_s[phase, H - 1 + s] for s in range(cx + 2)]
        ts = [a[0:cy] for a in t]
        dz = [zhigh(a) - zlow(a) for a in t]
        dy = [(yhigh(a) - ylow(a))[0:cy] for a in t]
        out = []
        qx = []
        for x in range(cx + 1):
            qx.append(
                kx_s[0, x] * (ts[x + 1] - ts[x])
                + kx_s[1, x] * (dy[x] + dy[x + 1])
                + kx_s[2, x] * (dz[x] + dz[x + 1])[0:cy]
            )
        for x in range(cx):
            a = t[x + 1]
            dx = t[x + 2] - t[x]
            qy = (
                ky_s[1, x] * (a - ylow(a))
                + ky_s[0, x] * (dx + ylow(dx))
                + ky_s[2, x] * (dz[x + 1] + ylow(dz[x + 1]))
            )
            dxs = dx[0:cy]
            qz = (
                kz_s[2, x] * (ts[x + 1] - zlow(ts[x + 1]))
                + kz_s[0, x] * (dxs + zlow(dxs))
                + kz_s[1, x] * (dy[x + 1] + zlow(dy[x + 1]))
            )
            out.append(qx[x + 1] - qx[x] + (yhigh(qy) - qy)[0:cy] + (zhigh(qz) - qz))
        return jnp.stack(out)

    first_factor, factors = rkl_factors()
    inner = pl.ds(H, cx)
    base = e_s[inner, 0:cy, :]
    irho = irho_s[inner, 0:cy, :]
    rate0 = rate(0)
    earlier, latest = base, base + first_factor * rate0
    for n, (mu, nu, rest, fresh, zero) in enumerate(factors):
        phase = n + 1
        t = latest * irho
        for x in range(cx):
            pk[n, 0, x : x + 1, :] = t[x, cy - 1 : cy, :]
            pk[n, 1, x : x + 1, :] = t[x, 0:1, :]
        t_s[phase, inner, 0:cy, :] = t
        copies = []
        for k, (dx, dy) in enumerate(ring):
            if dy == 1:
                copies.append(remote(phase, k, pk.at[n, 0], low_row.at[n, dx + 1]))
            elif dy == -1:
                copies.append(remote(phase, k, pk.at[n, 1], high_row.at[n, dx + 1]))
            else:
                src = H + cx - 1 if dx == 1 else H
                dst = H - 1 if dx == 1 else H + cx
                copies.append(
                    remote(
                        phase, k,
                        t_s.at[phase, src, pl.ds(0, cy)],
                        t_s.at[phase, dst, pl.ds(0, cy)],
                    )
                )
        part = mu * latest + nu * earlier + rest * base + zero * rate0
        sent += copies
        for copy in copies:
            copy.wait_recv()
        for s in range(cx + 2):
            if s == 0:
                d, x = 2, cx - 1
            elif s == cx + 1:
                d, x = 0, 0
            else:
                d, x = 1, s - 1
            t_s[phase, H - 1 + s, cy : cy + 1, :] = high_row[n, d, x : x + 1, :]
            t_s[phase, H - 1 + s, ROWS - 1 : ROWS, :] = low_row[n, d, x : x + 1, :]
        earlier, latest = latest, part + fresh * rate(phase)
    o_p[...] = (G - 1.0) * latest
    stores.append(pltpu.make_async_copy(o_p, p_out, out_sem.at[3]))
    stores[3].start()
    for copy in sent:
        copy.wait_send()
    for store in stores:
        store.wait()


def hand_on(*refs):
    copies = [
        pltpu.make_async_copy(refs[n], refs[4 + n], refs[8].at[n]) for n in range(4)
    ]
    for copy in copies:
        copy.start()
    for copy in copies:
        copy.wait()


def solution(mesh):
    nx, ny = mesh.shape["gx"], mesh.shape["gy"]

    def local(rho, v, p, b):
        cx, cy, nz = rho.shape
        wide = cx + 2 * H
        f32 = jnp.float32
        vm = lambda *shape: pltpu.VMEM(shape, f32)
        phases = SECTIONS - 1
        spec = pl.BlockSpec(memory_space=pl.ANY)
        shapes = [jax.ShapeDtypeStruct(a.shape, f32) for a in (rho, v, p, b)]
        results = pl.pallas_call(
            functools.partial(kernel, nx, ny),
            out_shape=shapes,
            in_specs=[pl.BlockSpec(memory_space=pltpu.HBM)] * 4,
            out_specs=[spec] * 4,
            scratch_shapes=[
                vm(cx, cy, nz),
                vm(3, cx, cy, nz),
                vm(cx, cy, nz),
                vm(3, cx, cy, nz),
                vm(8, wide, ROWS, nz),
                vm(cx, 8 * H, nz),
                vm(cx, 8 * H, nz),
                vm(wide, 8 * H, nz),
                vm(wide, 8 * H, nz),
                vm(7, ROWS, nz),
                vm(7, ROWS, nz),
                vm(2, ROWS, nz),
                vm(5, ROWS, nz),
                vm(2, ROWS, nz),
                vm(3, ROWS, nz),
                vm(wide, ROWS, nz),
                vm(wide, ROWS, nz),
                vm(wide, ROWS, nz),
                vm(3, wide, ROWS, nz),
                vm(3, wide, ROWS, nz),
                vm(3, cx + 1, cy, nz),
                vm(3, cx + 1, ROWS, nz),
                vm(3, cx + 1, cy, nz),
                vm(SECTIONS, wide, ROWS, nz),
                vm(phases, 2, cx, nz),
                vm(phases, 3, cx, nz),
                vm(phases, 3, cx, nz),
                pltpu.SemaphoreType.DMA((SECTIONS, 8)),
                pltpu.SemaphoreType.DMA((SECTIONS, 8)),
                pltpu.SemaphoreType.DMA((4,)),
                pltpu.SemaphoreType.DMA((4,)),
            ],
            compiler_params=pltpu.CompilerParams(collective_id=0, has_side_effects=True),
        )(rho, v, p, b)
        return pl.pallas_call(
            hand_on,
            out_shape=shapes,
            in_specs=[spec] * 4,
            out_specs=[spec] * 4,
            scratch_shapes=[pltpu.SemaphoreType.DMA((4,))],
        )(*results)

    placed = (
        P("gx", "gy", None),
        P(None, "gx", "gy", None),
        P("gx", "gy", None),
        P(None, "gx", "gy", None),
    )
    return jax.shard_map(
        lambda *a: tuple(local(*a)),
        mesh=mesh,
        in_specs=placed,
        out_specs=placed,
        check_vma=False,
    )
```

```python
import functools

import jax
import jax.numpy as jnp
from jax import lax
from jax.experimental import pallas as pl
from jax.experimental.pallas import tpu as pltpu
from jax.sharding import PartitionSpec as P

SECTIONS = 4
SUPER_SECTIONS = 8

G = 5.0 / 3.0
DT = 0.04
SUPER_TIME = 0.08
DENSITY_FLOOR = 0.5
PRESSURE_FLOOR = 0.1
FIELD_FLOOR = 0.05

MESH = pl.DeviceIdType.MESH

H = 3
ROWS = 16


def ylow(a):
    return pltpu.roll(a, 1, 0)


def yhigh(a):
    return pltpu.roll(a, a.shape[0] - 1, 0)


def zlow(a):
    return pltpu.roll(a, 1, 1)


def zhigh(a):
    return pltpu.roll(a, a.shape[1] - 1, 1)


def minmod(a, b):
    return jnp.maximum(jnp.minimum(a, b), 0.0) + jnp.minimum(jnp.maximum(a, b), 0.0)


def wave(rho, v, p, b, d):
    bsq = b[0] * b[0] + b[1] * b[1] + b[2] * b[2]
    ksq = v[0] * v[0] + v[1] * v[1] + v[2] * v[2]
    half = 0.5 * bsq
    energy = p * 1.5 + 0.5 * rho * ksq + half
    total = p + half
    vn, bn = v[d], b[d]
    proj = v[0] * b[0] + v[1] * b[1] + v[2] * b[2]
    others = [c for c in range(3) if c != d]
    m = [rho * v[c] for c in range(3)]
    cons = [rho] + m + [energy] + [b[c] for c in others]
    mom = []
    for c in range(3):
        t = m[d] * v[c] - bn * b[c]
        mom.append(t + total if c == d else t)
    flux = [m[d]] + mom + [(energy + total) * vn - bn * proj]
    flux += [vn * b[c] - v[c] * bn for c in others]
    a = G * p + bsq
    signal = jnp.abs(vn) + a * lax.rsqrt(a * rho)
    return cons, flux, signal


def face_flux(lower, upper, bn, d):
    def split(s):
        rest = list(s[5:])
        rest.insert(d, bn)
        return s[0], s[1:4], s[4], rest

    ul, fl, sl = wave(*split(lower), d)
    uu, fu, su = wave(*split(upper), d)
    signal = jnp.maximum(sl, su)
    return [0.5 * ((fl[n] + fu[n]) - signal * (uu[n] - ul[n])) for n in range(7)]


def along(prims, bn, d):
    low, high = (ylow, yhigh) if d == 1 else (zlow, zhigh)
    lower, upper = [], []
    for q in prims:
        diff = q - low(q)
        half = 0.5 * minmod(diff, high(diff))
        lower.append(low(q + half))
        upper.append(q - half)
    return face_flux(lower, upper, bn, d)


def rkl_factors():
    b = [1.0 / 3.0] * 3 + [
        (j * j + j - 2.0) / (2.0 * j * (j + 1.0)) for j in range(3, SUPER_SECTIONS + 1)
    ]
    w = 4.0 / (SUPER_SECTIONS * SUPER_SECTIONS + SUPER_SECTIONS - 2.0)
    rows = []
    for j in range(2, SECTIONS + 1):
        mu = (2.0 * j - 1.0) / j * b[j] / b[j - 1]
        nu = -(j - 1.0) / j * b[j] / b[j - 2]
        rate = mu * w * SUPER_TIME
        rows.append((mu, nu, 1.0 - mu - nu, rate, -(1.0 - b[j - 1]) * rate))
    return b[1] * w * SUPER_TIME, rows


def kernel(
    nx, ny,
    rho_ref, v_ref, p_ref, b_ref,
    rho_out, v_out, p_out, b_out,
    o_rho, o_v, o_p, o_b,
    ext, up, down, from_low, from_high,
    cell, fx_s, fy_s, fz_s, b_s,
    irho_s, e_s, kap_s, bc_s, bf_s, kx_s, ky_s, kz_s,
    t_s, pk, low_row, high_row,
    send_sem, recv_sem, in_sem, out_sem,
):
    cx, cy = o_rho.shape[0], o_rho.shape[1]
    gx, gy = lax.axis_index("gx"), lax.axis_index("gy")

    def target(dx, dy):
        return (lax.rem(gx + dx + nx, nx), lax.rem(gy + dy + ny, ny))

    ring = [(dx, dy) for dy in (1, -1, 0) for dx in (0, 1, -1) if (dx, dy) != (0, 0)]

    barrier = pltpu.get_barrier_semaphore()
    for dx, dy in ring:
        pl.semaphore_signal(barrier, inc=1, device_id=target(dx, dy), device_id_type=MESH)

    own, near = pl.ds(H, cx), pl.ds(0, cy)
    places = [
        (rho_ref, ext.at[0, own, near]),
        (v_ref, ext.at[pl.ds(1, 3), own, near]),
        (p_ref, ext.at[4, own, near]),
        (b_ref, ext.at[pl.ds(5, 3), own, near]),
    ]
    loads = [
        pltpu.make_async_copy(src, dst, in_sem.at[n]) for n, (src, dst) in enumerate(places)
    ]
    for load in loads:
        load.start()
    for load in loads:
        load.wait()
    for f in range(8):
        value = ext[f, H : H + cx, 0:cy, :]
        up[:, H * f : H * f + H, :] = value[:, cy - H : cy, :]
        down[:, H * f : H * f + H, :] = value[:, 0:H, :]
    pl.semaphore_wait(barrier, len(ring))

    def remote(phase, k, src, dst, to=None):
        copy = pltpu.make_async_remote_copy(
            src_ref=src,
            dst_ref=dst,
            send_sem=send_sem.at[phase, k],
            recv_sem=recv_sem.at[phase, k],
            device_id=target(*(to or ring[k])),
            device_id_type=MESH,
        )
        copy.start()
        return copy

    def side(k):
        return ring.index(k)

    wide = cx + 2 * H
    mine, low3, high3 = pl.ds(H, cx), pl.ds(0, H), pl.ds(H + cx, H)
    first3, last3 = pl.ds(H, H), pl.ds(cx, H)

    to_high = remote(0, side((0, 1)), up, from_low.at[mine])
    to_low = remote(0, side((0, -1)), down, from_high.at[mine])
    slabs = [
        remote(0, side((1, 0)), ext.at[:, last3, near], ext.at[:, low3, near]),
        remote(0, side((-1, 0)), ext.at[:, first3, near], ext.at[:, high3, near]),
    ]
    sent = [to_high, to_low] + slabs

    one = jnp.ones((ROWS, 128), jnp.float32)
    for n in range(3):
        b_s[n] = one
    for f in range(8):
        ext[f, :, cy:ROWS, :] = jnp.ones((wide, ROWS - cy, 128), jnp.float32)

    A, B, BOTH = slice(0, cy), slice(cy, ROWS), slice(0, ROWS)

    def cells_own(s, e):
        bx, by, bz = (ext[5 + c, s:e, A] for c in range(3))
        nx_, nz_ = ext[5, s + 1 : e + 1, A], pltpu.roll(bz, 127, 2)
        cell[0, s:e, A] = 0.5 * (bx + nx_)
        cell[1, s:e, A] = by - 0.5 * ((nx_ - bx) + (nz_ - bz))
        cell[2, s:e, A] = 0.5 * (bz + nz_)

    def cell_x(s, e):
        cell[0, s:e, B] = 0.5 * (ext[5, s:e, B] + ext[5, s + 1 : e + 1, B])

    def cell_yz(s, e, rows):
        for x in range(s, e):
            by, bz = ext[6, x], ext[7, x, rows]
            cell[1, x, rows] = (0.5 * (by + yhigh(by)))[rows]
            cell[2, x, rows] = 0.5 * (bz + zhigh(bz))

    def prims(s, rows, d):
        return [ext[f, s, rows] for f in range(5)] + [
            cell[c, s, rows] for c in range(3) if c != d
        ]

    def flux_z(s, rows):
        for n, a in enumerate(along(prims(s, rows, 2), ext[7, s, rows], 2)):
            fz_s[n, s, rows] = a

    def flux_y(s):
        for n, a in enumerate(along(prims(s, BOTH, 1), ext[6, s], 1)):
            fy_s[n, s] = a

    def flux_x(i, rows):
        q = [prims(i + o, rows, 0) for o in (-2, -1, 0, 1)]
        lower, upper = [], []
        for q0, q1, q2, q3 in zip(*q):
            d1 = q2 - q1
            lower.append(q1 + 0.5 * minmod(q1 - q0, d1))
            upper.append(q2 - 0.5 * minmod(d1, q3 - q2))
        for n, a in enumerate(face_flux(lower, upper, ext[5, i, rows], 0)):
            fx_s[n, i, rows] = a

    def loop(count, f, unroll):
        def step(k, carry):
            f(k)
            return carry

        lax.fori_loop(0, count, step, 0, unroll=unroll)

    def outer(k):
        return k + 1 + (cx - 1) * ((k + 3) // 5)

    cells_own(H, H + cx - 1)
    loop(cx - 1, lambda k: flux_z(H + k, A), cx - 1)
    for copy in slabs:
        copy.wait_recv()
    cells_own(0, H)
    cells_own(H + cx - 1, wide - 1)
    loop(5, lambda k: flux_z(outer(k), A), 5)
    loop(cx + 2, lambda k: flux_x(2 + k, A), 2)

    corners = []
    for copy, dy, buffer in ((to_high, 1, from_low), (to_low, -1, from_high)):
        copy.wait_recv()
        corners.append(remote(0, side((1, dy)), buffer.at[last3], buffer.at[low3], (1, 0)))
        corners.append(remote(0, side((-1, dy)), buffer.at[first3], buffer.at[high3], (-1, 0)))
    sent += corners

    def unpack(s, e):
        for f in range(8):
            ext[f, s:e, cy : cy + H, :] = from_high[s:e, H * f : H * f + H, :]
            ext[f, s:e, ROWS - H : ROWS, :] = from_low[s:e, H * f : H * f + H, :]

    unpack(H, H + cx)
    cell_x(H, H + cx - 1)
    cell_yz(H, H + cx, B)

    def middle(k):
        flux_y(H + k)
        flux_z(H + k, B)

    loop(cx - 1, middle, 1)
    loop(cx - 3, lambda k: flux_x(H + 2 + k, B), cx - 3)

    for copy in corners:
        copy.wait_recv()
    unpack(0, H)
    unpack(H + cx, wide)
    cell_x(0, H)
    cell_x(H + cx - 1, wide - 1)
    cell_yz(0, H, B)
    cell_yz(H + cx, wide - 1, B)
    cell_yz(wide - 1, wide, BOTH)

    def ends(k):
        flux_y(outer(k))
        flux_z(outer(k), B)

    loop(5, ends, 1)
    loop(6, lambda k: flux_x(2 + k + (cx - 3) * (k // 3), B), 2)
    flux_x(wide - 2, A)

    def body(i):
        bx, by, bz = ext[5, i], ext[6, i], ext[7, i]
        xy, xz = fx_s[5, i], fx_s[6, i]
        yx, yz = fy_s[5, i], fy_s[6, i]
        zx, zy = fz_s[5, i], fz_s[6, i]
        ez = 0.25 * (fy_s[5, i - 1] + yx - ylow(xy) - xy)
        ey = 0.25 * (zlow(xz) + xz - fz_s[5, i - 1] - zx)
        ex = 0.25 * (ylow(zy) + zy - zlow(yz) - yz)
        bxn = bx - DT * (yhigh(ez) - ez) + DT * (zhigh(ey) - ey)
        bxo = b_s[0]
        byn = b_s[1] + DT * ez
        bzn = b_s[2] - DT * ey
        b_s[0] = bxn
        b_s[1] = by - DT * (zhigh(ex) - ex) - DT * ez
        b_s[2] = bz + DT * ey + DT * (yhigh(ex) - ex)

        m = i - 1
        rho, v, p = ext[0, m], [ext[1 + c, m] for c in range(3)], ext[4, m]
        bm = [cell[c, m] for c in range(3)]
        energy = (
            p * 1.5
            + 0.5 * rho * (v[0] * v[0] + v[1] * v[1] + v[2] * v[2])
            + 0.5 * (bm[0] * bm[0] + bm[1] * bm[1] + bm[2] * bm[2])
        )
        new = [rho, rho * v[0], rho * v[1], rho * v[2], energy]
        for n in range(5):
            fy, fz = fy_s[n, m], fz_s[n, m]
            change = (yhigh(fy) - fy) + (zhigh(fz) - fz) + (fx_s[n, i] - fx_s[n, m])
            new[n] = new[n] - DT * change

        floored = jnp.maximum(new[0], DENSITY_FLOOR)
        inv = 1.0 / floored
        vel = [new[1 + c] * inv for c in range(3)]
        bc = [0.5 * (bxo + bxn), 0.5 * (byn + yhigh(byn)), 0.5 * (bzn + zhigh(bzn))]
        kinetic = new[1] * vel[0] + new[2] * vel[1] + new[3] * vel[2]
        internal = new[4] - 0.5 * kinetic - 0.5 * (bc[0] * bc[0] + bc[1] * bc[1] + bc[2] * bc[2])
        p1 = jnp.maximum((G - 1.0) * internal, PRESSURE_FLOOR)
        t = p1 * inv
        irho_s[m] = (G - 1.0) * inv
        e_s[m] = p1 * 1.5
        t_s[0, m] = t
        kap_s[m] = t * t * jnp.sqrt(t)
        for c in range(3):
            bc_s[c, m] = bc[c]
        for c, a in enumerate((bxo, byn, bzn)):
            bf_s[c, m] = a
        if isinstance(i, int):
            return
        x = jnp.maximum(m - H, 0)
        o_rho[x] = floored[A]
        for c in range(3):
            o_v[c, x] = vel[c][A]
        for c, a in enumerate((bxo, byn, bzn)):
            o_b[c, x] = a[A]

    loop(cx + 2, lambda k: body(2 + k), 2)
    body(wide - 2)
    stores = [
        pltpu.make_async_copy(src, dst, out_sem.at[n])
        for n, (src, dst) in enumerate(((o_rho, rho_out), (o_v, v_out), (o_b, b_out)))
    ]
    for store in stores:
        store.start()

    def coupling(s, carry):
        kap = kap_s[s]
        bc = [bc_s[c, s] for c in range(3)]
        bf = [bf_s[c, s] for c in range(3)]
        for d, out in enumerate((kx_s, ky_s, kz_s)):
            if d == 0:
                kl, bl = kap_s[s - 1], [bc_s[c, s - 1] for c in range(3)]
            else:
                low = ylow if d == 1 else zlow
                kl, bl = low(kap), [low(bc[c]) if c != d else None for c in range(3)]
            comp = [bf[d] if c == d else 0.5 * (bc[c] + bl[c]) for c in range(3)]
            mag = comp[0] * comp[0] + comp[1] * comp[1] + comp[2] * comp[2]
            factor = 0.5 * (kap + kl) / jnp.maximum(mag, FIELD_FLOOR) * bf[d]
            rows = ROWS if d == 1 else cy
            for c in range(3):
                k = factor * comp[c] * (1.0 if c == d else 0.25)
                out[c, s - H] = k[0:rows]
        return carry

    lax.fori_loop(H, H + cx + 1, coupling, 0, unroll=3)

    def rate(phase):
        t = [t_s[phase, H - 1 + s] for s in range(cx + 2)]
        ts = [a[0:cy] for a in t]
        dz = [zhigh(a) - zlow(a) for a in t]
        dy = [(yhigh(a) - ylow(a))[0:cy] for a in t]
        out = []
        qx = []
        for x in range(cx + 1):
            qx.append(
                kx_s[0, x] * (ts[x + 1] - ts[x])
                + kx_s[1, x] * (dy[x] + dy[x + 1])
                + kx_s[2, x] * (dz[x] + dz[x + 1])[0:cy]
            )
        for x in range(cx):
            a = t[x + 1]
            dx = t[x + 2] - t[x]
            qy = (
                ky_s[1, x] * (a - ylow(a))
                + ky_s[0, x] * (dx + ylow(dx))
                + ky_s[2, x] * (dz[x + 1] + ylow(dz[x + 1]))
            )
            dxs = dx[0:cy]
            qz = (
                kz_s[2, x] * (ts[x + 1] - zlow(ts[x + 1]))
                + kz_s[0, x] * (dxs + zlow(dxs))
                + kz_s[1, x] * (dy[x + 1] + zlow(dy[x + 1]))
            )
            out.append(qx[x + 1] - qx[x] + (yhigh(qy) - qy)[0:cy] + (zhigh(qz) - qz))
        return jnp.stack(out)

    first_factor, factors = rkl_factors()
    inner = pl.ds(H, cx)
    base = e_s[inner, 0:cy, :]
    irho = irho_s[inner, 0:cy, :]
    rate0 = rate(0)
    earlier, latest = base, base + first_factor * rate0
    for n, (mu, nu, rest, fresh, zero) in enumerate(factors):
        phase = n + 1
        t = latest * irho
        for x in range(cx):
            pk[n, 0, x : x + 1, :] = t[x, cy - 1 : cy, :]
            pk[n, 1, x : x + 1, :] = t[x, 0:1, :]
        t_s[phase, inner, 0:cy, :] = t
        copies = []
        for k, (dx, dy) in enumerate(ring):
            if dy == 1:
                copies.append(remote(phase, k, pk.at[n, 0], low_row.at[n, dx + 1]))
            elif dy == -1:
                copies.append(remote(phase, k, pk.at[n, 1], high_row.at[n, dx + 1]))
            else:
                src = H + cx - 1 if dx == 1 else H
                dst = H - 1 if dx == 1 else H + cx
                copies.append(
                    remote(
                        phase, k,
                        t_s.at[phase, src, pl.ds(0, cy)],
                        t_s.at[phase, dst, pl.ds(0, cy)],
                    )
                )
        part = mu * latest + nu * earlier + rest * base + zero * rate0
        sent += copies
        for copy in copies:
            copy.wait_recv()
        for s in range(cx + 2):
            if s == 0:
                d, x = 2, cx - 1
            elif s == cx + 1:
                d, x = 0, 0
            else:
                d, x = 1, s - 1
            t_s[phase, H - 1 + s, cy : cy + 1, :] = high_row[n, d, x : x + 1, :]
            t_s[phase, H - 1 + s, ROWS - 1 : ROWS, :] = low_row[n, d, x : x + 1, :]
        earlier, latest = latest, part + fresh * rate(phase)
    o_p[...] = (G - 1.0) * latest
    stores.append(pltpu.make_async_copy(o_p, p_out, out_sem.at[3]))
    stores[3].start()
    for copy in sent:
        copy.wait_send()
    for store in stores:
        store.wait()


def hand_on(*refs):
    source, result, held, in_sem, out_sem = refs[:4], refs[4:8], refs[8:12], refs[12], refs[13]
    loads = [pltpu.make_async_copy(source[n], held[n], in_sem.at[n]) for n in range(4)]
    stores = [pltpu.make_async_copy(held[n], result[n], out_sem.at[n]) for n in range(4)]
    for load in loads:
        load.start()
    for load, store in zip(loads, stores):
        load.wait()
        store.start()
    for store in stores:
        store.wait()


def solution(mesh):
    nx, ny = mesh.shape["gx"], mesh.shape["gy"]

    def local(rho, v, p, b):
        cx, cy, nz = rho.shape
        wide = cx + 2 * H
        f32 = jnp.float32
        vm = lambda *shape: pltpu.VMEM(shape, f32)
        phases = SECTIONS - 1
        spec = pl.BlockSpec(memory_space=pl.ANY)
        shapes = [jax.ShapeDtypeStruct(a.shape, f32) for a in (rho, v, p, b)]
        results = pl.pallas_call(
            functools.partial(kernel, nx, ny),
            out_shape=shapes,
            in_specs=[pl.BlockSpec(memory_space=pltpu.HBM)] * 4,
            out_specs=[spec] * 4,
            scratch_shapes=[
                vm(cx, cy, nz),
                vm(3, cx, cy, nz),
                vm(cx, cy, nz),
                vm(3, cx, cy, nz),
                vm(8, wide, ROWS, nz),
                vm(cx, 8 * H, nz),
                vm(cx, 8 * H, nz),
                vm(wide, 8 * H, nz),
                vm(wide, 8 * H, nz),
                vm(3, wide, ROWS, nz),
                vm(7, wide, ROWS, nz),
                vm(7, wide, ROWS, nz),
                vm(7, wide, ROWS, nz),
                vm(3, ROWS, nz),
                vm(wide, ROWS, nz),
                vm(wide, ROWS, nz),
                vm(wide, ROWS, nz),
                vm(3, wide, ROWS, nz),
                vm(3, wide, ROWS, nz),
                vm(3, cx + 1, cy, nz),
                vm(3, cx + 1, ROWS, nz),
                vm(3, cx + 1, cy, nz),
                vm(SECTIONS, wide, ROWS, nz),
                vm(phases, 2, cx, nz),
                vm(phases, 3, cx, nz),
                vm(phases, 3, cx, nz),
                pltpu.SemaphoreType.DMA((SECTIONS, 8)),
                pltpu.SemaphoreType.DMA((SECTIONS, 8)),
                pltpu.SemaphoreType.DMA((4,)),
                pltpu.SemaphoreType.DMA((4,)),
            ],
            compiler_params=pltpu.CompilerParams(collective_id=0, has_side_effects=True),
        )(rho, v, p, b)
        return pl.pallas_call(
            hand_on,
            out_shape=shapes,
            in_specs=[spec] * 4,
            out_specs=[spec] * 4,
            scratch_shapes=[vm(*a.shape) for a in shapes]
            + [pltpu.SemaphoreType.DMA((4,)), pltpu.SemaphoreType.DMA((4,))],
        )(*results)

    placed = (
        P("gx", "gy", None),
        P(None, "gx", "gy", None),
        P("gx", "gy", None),
        P(None, "gx", "gy", None),
    )
    return jax.shard_map(
        lambda *a: tuple(local(*a)),
        mesh=mesh,
        in_specs=placed,
        out_specs=placed,
        check_vma=False,
    )
```

```python
import functools

import jax
import jax.numpy as jnp
from jax import lax
from jax.experimental import pallas as pl
from jax.experimental.pallas import tpu as pltpu
from jax.sharding import PartitionSpec as P

SECTIONS = 4
SUPER_SECTIONS = 8

G = 5.0 / 3.0
DT = 0.04
SUPER_TIME = 0.08
DENSITY_FLOOR = 0.5
PRESSURE_FLOOR = 0.1
FIELD_FLOOR = 0.05

MESH = pl.DeviceIdType.MESH

H = 4
ROWS = 16


def ylow(a):
    return pltpu.roll(a, 1, 0)


def yhigh(a):
    return pltpu.roll(a, a.shape[0] - 1, 0)


def zlow(a):
    return pltpu.roll(a, 1, 1)


def zhigh(a):
    return pltpu.roll(a, a.shape[1] - 1, 1)


def minmod(a, b):
    return jnp.maximum(jnp.minimum(a, b), 0.0) + jnp.minimum(jnp.maximum(a, b), 0.0)


def wave(rho, v, p, b, d):
    bsq = b[0] * b[0] + b[1] * b[1] + b[2] * b[2]
    ksq = v[0] * v[0] + v[1] * v[1] + v[2] * v[2]
    half = 0.5 * bsq
    energy = p * 1.5 + 0.5 * rho * ksq + half
    total = p + half
    vn, bn = v[d], b[d]
    proj = v[0] * b[0] + v[1] * b[1] + v[2] * b[2]
    others = [c for c in range(3) if c != d]
    m = [rho * v[c] for c in range(3)]
    cons = [rho] + m + [energy] + [b[c] for c in others]
    mom = []
    for c in range(3):
        t = m[d] * v[c] - bn * b[c]
        mom.append(t + total if c == d else t)
    flux = [m[d]] + mom + [(energy + total) * vn - bn * proj]
    flux += [vn * b[c] - v[c] * bn for c in others]
    a = G * p + bsq
    signal = jnp.abs(vn) + a * lax.rsqrt(a * rho)
    return cons, flux, signal


def face_flux(lower, upper, bn, d):
    def split(s):
        rest = list(s[5:])
        rest.insert(d, bn)
        return s[0], s[1:4], s[4], rest

    ul, fl, sl = wave(*split(lower), d)
    uu, fu, su = wave(*split(upper), d)
    signal = jnp.maximum(sl, su)
    return [0.5 * ((fl[n] + fu[n]) - signal * (uu[n] - ul[n])) for n in range(7)]


def along(prims, bn, d):
    low, high = (ylow, yhigh) if d == 1 else (zlow, zhigh)
    lower, upper = [], []
    for q in prims:
        diff = q - low(q)
        half = 0.5 * minmod(diff, high(diff))
        lower.append(low(q + half))
        upper.append(q - half)
    return face_flux(lower, upper, bn, d)


def rkl_factors():
    b = [1.0 / 3.0] * 3 + [
        (j * j + j - 2.0) / (2.0 * j * (j + 1.0)) for j in range(3, SUPER_SECTIONS + 1)
    ]
    w = 4.0 / (SUPER_SECTIONS * SUPER_SECTIONS + SUPER_SECTIONS - 2.0)
    rows = []
    for j in range(2, SECTIONS + 1):
        mu = (2.0 * j - 1.0) / j * b[j] / b[j - 1]
        nu = -(j - 1.0) / j * b[j] / b[j - 2]
        rate = mu * w * SUPER_TIME
        rows.append((mu, nu, 1.0 - mu - nu, rate, -(1.0 - b[j - 1]) * rate))
    return b[1] * w * SUPER_TIME, rows


def kernel(
    nx, ny,
    rho_ref, v_ref, p_ref, b_ref,
    rho_out, v_out, p_out, b_out,
    o_rho, o_v, o_p, o_b,
    ext, up, down, from_low, from_high,
    cell, fx_s, fy_s, fz_s, b_s,
    irho_s, kap_s, bc_s, bf_s, kx_s, ky_s, kz_s,
    t_s, r_s, pk, low_row, high_row,
    send_sem, recv_sem, in_sem, out_sem,
):
    cx, cy = o_rho.shape[0], o_rho.shape[1]
    gx, gy = lax.axis_index("gx"), lax.axis_index("gy")

    def target(dx, dy):
        return (lax.rem(gx + dx + nx, nx), lax.rem(gy + dy + ny, ny))

    ring = [(dx, dy) for dy in (1, -1, 0) for dx in (0, 1, -1) if (dx, dy) != (0, 0)]

    barrier = pltpu.get_barrier_semaphore()
    for dx, dy in ring:
        pl.semaphore_signal(barrier, inc=1, device_id=target(dx, dy), device_id_type=MESH)

    own, near = pl.ds(H, cx), pl.ds(0, cy)
    places = [
        (rho_ref, ext.at[0, own, near]),
        (v_ref, ext.at[pl.ds(1, 3), own, near]),
        (p_ref, ext.at[4, own, near]),
        (b_ref, ext.at[pl.ds(5, 3), own, near]),
    ]
    loads = [
        pltpu.make_async_copy(src, dst, in_sem.at[n]) for n, (src, dst) in enumerate(places)
    ]
    for load in loads:
        load.start()
    for load in loads:
        load.wait()
    for f in range(8):
        value = ext[f, H : H + cx, 0:cy, :]
        up[:, H * f : H * f + H, :] = value[:, cy - H : cy, :]
        down[:, H * f : H * f + H, :] = value[:, 0:H, :]
    pl.semaphore_wait(barrier, len(ring))

    def remote(phase, k, src, dst, to=None):
        copy = pltpu.make_async_remote_copy(
            src_ref=src,
            dst_ref=dst,
            send_sem=send_sem.at[phase, k],
            recv_sem=recv_sem.at[phase, k],
            device_id=target(*(to or ring[k])),
            device_id_type=MESH,
        )
        copy.start()
        return copy

    def side(k):
        return ring.index(k)

    wide = cx + 2 * H
    mine, low_h, high_h = pl.ds(H, cx), pl.ds(0, H), pl.ds(H + cx, H)
    first_h, last_h = pl.ds(H, H), pl.ds(cx, H)

    to_high = remote(0, side((0, 1)), up, from_low.at[mine])
    to_low = remote(0, side((0, -1)), down, from_high.at[mine])
    slabs = [
        remote(0, side((1, 0)), ext.at[:, last_h, near], ext.at[:, low_h, near]),
        remote(0, side((-1, 0)), ext.at[:, first_h, near], ext.at[:, high_h, near]),
    ]
    sent = [to_high, to_low] + slabs

    one = jnp.ones((ROWS, 128), jnp.float32)
    for n in range(3):
        b_s[n] = one

    A, B, BOTH = slice(0, cy), slice(cy, ROWS), slice(0, ROWS)

    def cells_own(s, e):
        bx, by, bz = (ext[5 + c, s:e, A] for c in range(3))
        nx_, nz_ = ext[5, s + 1 : e + 1, A], pltpu.roll(bz, 127, 2)
        cell[0, s:e, A] = 0.5 * (bx + nx_)
        cell[1, s:e, A] = by - 0.5 * ((nx_ - bx) + (nz_ - bz))
        cell[2, s:e, A] = 0.5 * (bz + nz_)

    def cell_x(s, e):
        cell[0, s:e, B] = 0.5 * (ext[5, s:e, B] + ext[5, s + 1 : e + 1, B])

    def cell_yz(s, e, rows):
        for x in range(s, e):
            by, bz = ext[6, x], ext[7, x, rows]
            cell[1, x, rows] = (0.5 * (by + yhigh(by)))[rows]
            cell[2, x, rows] = 0.5 * (bz + zhigh(bz))

    def prims(s, rows, d):
        return [ext[f, s, rows] for f in range(5)] + [
            cell[c, s, rows] for c in range(3) if c != d
        ]

    def flux_z(s, rows):
        for n, a in enumerate(along(prims(s, rows, 2), ext[7, s, rows], 2)):
            fz_s[n, s, rows] = a

    def flux_y(s):
        for n, a in enumerate(along(prims(s, BOTH, 1), ext[6, s], 1)):
            fy_s[n, s] = a

    def flux_x(i, rows):
        q = [prims(i + o, rows, 0) for o in (-2, -1, 0, 1)]
        lower, upper = [], []
        for q0, q1, q2, q3 in zip(*q):
            d1 = q2 - q1
            lower.append(q1 + 0.5 * minmod(q1 - q0, d1))
            upper.append(q2 - 0.5 * minmod(d1, q3 - q2))
        for n, a in enumerate(face_flux(lower, upper, ext[5, i, rows], 0)):
            fx_s[n, i, rows] = a

    def loop(count, f, unroll):
        def step(k, carry):
            f(k)
            return carry

        lax.fori_loop(0, count, step, 0, unroll=unroll)

    def outer(k):
        return k + 1 + (cx - 1) * ((k + cx - H) // (cx - 1))

    cells_own(H, H + cx - 1)
    loop(cx - 1, lambda k: flux_z(H + k, A), cx - 1)
    for copy in slabs:
        copy.wait_recv()
    cells_own(0, H)
    cells_own(H + cx - 1, wide - 1)
    loop(cx - 1, lambda k: flux_z(outer(k), A), cx - 1)
    loop(cx + 4, lambda k: flux_x(2 + k, A), 2)

    corners = []
    for copy, dy, buffer in ((to_high, 1, from_low), (to_low, -1, from_high)):
        copy.wait_recv()
        corners.append(remote(0, side((1, dy)), buffer.at[last_h], buffer.at[low_h], (1, 0)))
        corners.append(remote(0, side((-1, dy)), buffer.at[first_h], buffer.at[high_h], (-1, 0)))
    sent += corners

    def unpack(s, e):
        for f in range(8):
            ext[f, s:e, cy : cy + H, :] = from_high[s:e, H * f : H * f + H, :]
            ext[f, s:e, ROWS - H : ROWS, :] = from_low[s:e, H * f : H * f + H, :]

    unpack(H, H + cx)
    cell_x(H, H + cx - 1)
    cell_yz(H, H + cx, B)

    def middle(k):
        flux_y(H + k)
        flux_z(H + k, B)

    loop(cx - 1, middle, 1)
    loop(cx - 3, lambda k: flux_x(H + 2 + k, B), cx - 3)

    for copy in corners:
        copy.wait_recv()
    unpack(0, H)
    unpack(H + cx, wide)
    cell_x(0, H)
    cell_x(H + cx - 1, wide - 1)
    cell_yz(0, H, B)
    cell_yz(H + cx, wide - 1, B)
    cell_yz(wide - 1, wide, BOTH)

    def ends(k):
        flux_y(outer(k))
        flux_z(outer(k), B)

    loop(cx - 1, ends, 1)
    loop(2 * H, lambda k: flux_x(2 + k + (cx - 3) * (k // H), B), 2)
    flux_x(wide - 2, A)

    def body(i):
        bx, by, bz = ext[5, i], ext[6, i], ext[7, i]
        xy, xz = fx_s[5, i], fx_s[6, i]
        yx, yz = fy_s[5, i], fy_s[6, i]
        zx, zy = fz_s[5, i], fz_s[6, i]
        ez = 0.25 * (fy_s[5, i - 1] + yx - ylow(xy) - xy)
        ey = 0.25 * (zlow(xz) + xz - fz_s[5, i - 1] - zx)
        ex = 0.25 * (ylow(zy) + zy - zlow(yz) - yz)
        bxn = bx - DT * (yhigh(ez) - ez) + DT * (zhigh(ey) - ey)
        bxo = b_s[0]
        byn = b_s[1] + DT * ez
        bzn = b_s[2] - DT * ey
        b_s[0] = bxn
        b_s[1] = by - DT * (zhigh(ex) - ex) - DT * ez
        b_s[2] = bz + DT * ey + DT * (yhigh(ex) - ex)

        m = i - 1
        rho, v, p = ext[0, m], [ext[1 + c, m] for c in range(3)], ext[4, m]
        bm = [cell[c, m] for c in range(3)]
        energy = (
            p * 1.5
            + 0.5 * rho * (v[0] * v[0] + v[1] * v[1] + v[2] * v[2])
            + 0.5 * (bm[0] * bm[0] + bm[1] * bm[1] + bm[2] * bm[2])
        )
        new = [rho, rho * v[0], rho * v[1], rho * v[2], energy]
        for n in range(5):
            fy, fz = fy_s[n, m], fz_s[n, m]
            change = (yhigh(fy) - fy) + (zhigh(fz) - fz) + (fx_s[n, i] - fx_s[n, m])
            new[n] = new[n] - DT * change

        floored = jnp.maximum(new[0], DENSITY_FLOOR)
        inv = 1.0 / floored
        vel = [new[1 + c] * inv for c in range(3)]
        bc = [0.5 * (bxo + bxn), 0.5 * (byn + yhigh(byn)), 0.5 * (bzn + zhigh(bzn))]
        kinetic = new[1] * vel[0] + new[2] * vel[1] + new[3] * vel[2]
        internal = new[4] - 0.5 * kinetic - 0.5 * (bc[0] * bc[0] + bc[1] * bc[1] + bc[2] * bc[2])
        p1 = jnp.maximum((G - 1.0) * internal, PRESSURE_FLOOR)
        t = p1 * inv
        irho_s[m] = (G - 1.0) * inv
        t_s[0, m] = t
        kap_s[m] = t * t * jnp.sqrt(t)
        for c in range(3):
            bc_s[c, m] = bc[c]
        for c, a in enumerate((bxo, byn, bzn)):
            bf_s[c, m] = a
        if isinstance(i, int):
            return
        x = jnp.maximum(m - H, 0)
        o_rho[x] = floored[A]
        for c in range(3):
            o_v[c, x] = vel[c][A]
        for c, a in enumerate((bxo, byn, bzn)):
            o_b[c, x] = a[A]

    body(2)
    loop(cx + 2, lambda k: body(3 + k), 2)
    body(wide - 3)
    body(wide - 2)
    stores = [
        pltpu.make_async_copy(src, dst, out_sem.at[n])
        for n, (src, dst) in enumerate(((o_rho, rho_out), (o_v, v_out), (o_b, b_out)))
    ]
    for store in stores:
        store.start()

    def coupling(s, carry):
        kap = kap_s[s]
        bc = [bc_s[c, s] for c in range(3)]
        bf = [bf_s[c, s] for c in range(3)]
        for d, out in enumerate((kx_s, ky_s, kz_s)):
            if d == 0:
                kl, bl = kap_s[s - 1], [bc_s[c, s - 1] for c in range(3)]
            else:
                low = ylow if d == 1 else zlow
                kl, bl = low(kap), [low(bc[c]) if c != d else None for c in range(3)]
            comp = [bf[d] if c == d else 0.5 * (bc[c] + bl[c]) for c in range(3)]
            mag = comp[0] * comp[0] + comp[1] * comp[1] + comp[2] * comp[2]
            factor = 0.5 * (kap + kl) / jnp.maximum(mag, FIELD_FLOOR) * bf[d]
            for c in range(3):
                out[c, s - H + 1] = factor * comp[c] * (1.0 if c == d else 0.25)
        return carry

    coupling(H - 1, 0)
    lax.fori_loop(H, H + cx + 2, coupling, 0, unroll=2)

    def rate(n, rim):
        rows = BOTH if rim else A
        t = {x: t_s[n, H + x] for x in range(-1 - rim, cx + 1 + rim)}
        dz = {x: zhigh(a) - zlow(a) for x, a in t.items()}
        dy = {x: (yhigh(a) - ylow(a))[rows] for x, a in t.items()}
        qx = {}
        for x in range(-rim, cx + 1 + rim):
            qx[x] = (
                kx_s[0, x + 1, rows] * (t[x] - t[x - 1])[rows]
                + kx_s[1, x + 1, rows] * (dy[x - 1] + dy[x])
                + kx_s[2, x + 1, rows] * (dz[x - 1] + dz[x])[rows]
            )
        out = []
        for x in range(-rim, cx + rim):
            a, dx, z = t[x], t[x + 1] - t[x - 1], dz[x]
            qy = (
                ky_s[1, x + 1] * (a - ylow(a))
                + ky_s[0, x + 1] * (dx + ylow(dx))
                + ky_s[2, x + 1] * (z + ylow(z))
            )
            a, dx, y = a[rows], dx[rows], dy[x]
            qz = (
                kz_s[2, x + 1, rows] * (a - zlow(a))
                + kz_s[0, x + 1, rows] * (dx + zlow(dx))
                + kz_s[1, x + 1, rows] * (y + zlow(y))
            )
            total = qx[x + 1] - qx[x] + (yhigh(qy) - qy)[rows] + (zhigh(qz) - qz)
            out.append(total * irho_s[H + x, rows])
        return jnp.stack(out)

    first_factor, factors = rkl_factors()
    inner, around = slice(H, H + cx), slice(H - 1, H + cx + 1)
    start = t_s[0, around]
    rate0 = rate(0, 1)
    r_s[...] = rate0
    t_s[1, around] = start + first_factor * rate0

    mu, nu, rest, fresh, zero = factors[0]
    second = (
        mu * t_s[1, inner, A]
        + (nu + rest) * t_s[0, inner, A]
        + zero * r_s[1 : cx + 1, A]
        + fresh * rate(1, 0)
    )
    for x in range(cx):
        for n in range(2):
            pk[0, n, x : x + 1, :] = second[x, cy - 2 + n : cy - 1 + n, :]
            pk[1, n, x : x + 1, :] = second[x, n : n + 1, :]
    t_s[2, inner, A] = second
    copies = []
    for k, (dx, dy) in enumerate(ring):
        if dy == 1:
            copies.append(remote(1, k, pk.at[0], low_row.at[dx + 1]))
        elif dy == -1:
            copies.append(remote(1, k, pk.at[1], high_row.at[dx + 1]))
        else:
            src = pl.ds(H + cx - 2 if dx == 1 else H, 2)
            dst = pl.ds(H - 2 if dx == 1 else H + cx, 2)
            copies.append(remote(1, k, t_s.at[2, src, near], t_s.at[2, dst, near]))
    mu, nu, rest, fresh, zero = factors[1]
    part = nu * t_s[1, around] + rest * t_s[0, around] + zero * r_s[...]
    for copy in copies:
        copy.wait_recv()
    sent += copies
    for x in range(-2, cx + 2):
        d = 2 if x < 0 else (0 if x >= cx else 1)
        row = x % cx
        for n in range(2):
            t_s[2, H + x, cy + n : cy + n + 1, :] = high_row[d, n, row : row + 1, :]
            t_s[2, H + x, ROWS - 2 + n : ROWS - 1 + n, :] = low_row[d, n, row : row + 1, :]
    t_s[3, around] = part + mu * t_s[2, around] + fresh * rate(2, 1)

    mu, nu, rest, fresh, zero = factors[2]
    last = (
        mu * t_s[3, inner, A]
        + nu * t_s[2, inner, A]
        + rest * t_s[0, inner, A]
        + zero * r_s[1 : cx + 1, A]
        + fresh * rate(3, 0)
    )
    o_p[...] = last * o_rho[...]
    stores.append(pltpu.make_async_copy(o_p, p_out, out_sem.at[3]))
    stores[3].start()
    for copy in sent:
        copy.wait_send()
    for store in stores:
        store.wait()


def hand_on(*refs):
    source, result, held, in_sem, out_sem = refs[:4], refs[4:8], refs[8:12], refs[12], refs[13]
    loads = [pltpu.make_async_copy(source[n], held[n], in_sem.at[n]) for n in range(4)]
    stores = [pltpu.make_async_copy(held[n], result[n], out_sem.at[n]) for n in range(4)]
    for load in loads:
        load.start()
    for load, store in zip(loads, stores):
        load.wait()
        store.start()
    for store in stores:
        store.wait()


def solution(mesh):
    nx, ny = mesh.shape["gx"], mesh.shape["gy"]

    def local(rho, v, p, b):
        cx, cy, nz = rho.shape
        wide = cx + 2 * H
        f32 = jnp.float32
        vm = lambda *shape: pltpu.VMEM(shape, f32)
        spec = pl.BlockSpec(memory_space=pl.ANY)
        shapes = [jax.ShapeDtypeStruct(a.shape, f32) for a in (rho, v, p, b)]
        results = pl.pallas_call(
            functools.partial(kernel, nx, ny),
            out_shape=shapes,
            in_specs=[pl.BlockSpec(memory_space=pltpu.HBM)] * 4,
            out_specs=[spec] * 4,
            scratch_shapes=[
                vm(cx, cy, nz),
                vm(3, cx, cy, nz),
                vm(cx, cy, nz),
                vm(3, cx, cy, nz),
                vm(8, wide, ROWS, nz),
                vm(cx, 8 * H, nz),
                vm(cx, 8 * H, nz),
                vm(wide, 8 * H, nz),
                vm(wide, 8 * H, nz),
                vm(3, wide, ROWS, nz),
                vm(7, wide, ROWS, nz),
                vm(7, wide, ROWS, nz),
                vm(7, wide, ROWS, nz),
                vm(3, ROWS, nz),
                vm(wide, ROWS, nz),
                vm(wide, ROWS, nz),
                vm(3, wide, ROWS, nz),
                vm(3, wide, ROWS, nz),
                vm(3, cx + 3, ROWS, nz),
                vm(3, cx + 3, ROWS, nz),
                vm(3, cx + 3, ROWS, nz),
                vm(SECTIONS, wide, ROWS, nz),
                vm(cx + 2, ROWS, nz),
                vm(2, 2, cx, nz),
                vm(3, 2, cx, nz),
                vm(3, 2, cx, nz),
                pltpu.SemaphoreType.DMA((2, 8)),
                pltpu.SemaphoreType.DMA((2, 8)),
                pltpu.SemaphoreType.DMA((4,)),
                pltpu.SemaphoreType.DMA((4,)),
            ],
            compiler_params=pltpu.CompilerParams(collective_id=0, has_side_effects=True),
        )(rho, v, p, b)
        return pl.pallas_call(
            hand_on,
            out_shape=shapes,
            in_specs=[spec] * 4,
            out_specs=[spec] * 4,
            scratch_shapes=[vm(*a.shape) for a in shapes]
            + [pltpu.SemaphoreType.DMA((4,)), pltpu.SemaphoreType.DMA((4,))],
        )(*results)

    placed = (
        P("gx", "gy", None),
        P(None, "gx", "gy", None),
        P("gx", "gy", None),
        P(None, "gx", "gy", None),
    )
    return jax.shard_map(
        lambda *a: tuple(local(*a)),
        mesh=mesh,
        in_specs=placed,
        out_specs=placed,
        check_vma=False,
    )
```

```python
import functools

import jax
import jax.numpy as jnp
from jax import lax
from jax.experimental import pallas as pl
from jax.experimental.pallas import tpu as pltpu
from jax.sharding import PartitionSpec as P

SECTIONS = 4
SUPER_SECTIONS = 8

G = 5.0 / 3.0
DT = 0.04
SUPER_TIME = 0.08
DENSITY_FLOOR = 0.5
PRESSURE_FLOOR = 0.1
FIELD_FLOOR = 0.05

MESH = pl.DeviceIdType.MESH

H = 4
ROWS = 16


def ylow(a):
    return pltpu.roll(a, 1, 0)


def yhigh(a):
    return pltpu.roll(a, a.shape[0] - 1, 0)


def zlow(a):
    return pltpu.roll(a, 1, 1)


def zhigh(a):
    return pltpu.roll(a, a.shape[1] - 1, 1)


def minmod(a, b):
    return jnp.maximum(jnp.minimum(a, b), 0.0) + jnp.minimum(jnp.maximum(a, b), 0.0)


def wave(rho, v, p, b, d):
    bsq = b[0] * b[0] + b[1] * b[1] + b[2] * b[2]
    ksq = v[0] * v[0] + v[1] * v[1] + v[2] * v[2]
    half = 0.5 * bsq
    energy = p * 1.5 + 0.5 * rho * ksq + half
    total = p + half
    vn, bn = v[d], b[d]
    proj = v[0] * b[0] + v[1] * b[1] + v[2] * b[2]
    others = [c for c in range(3) if c != d]
    m = [rho * v[c] for c in range(3)]
    cons = [rho] + m + [energy] + [b[c] for c in others]
    mom = []
    for c in range(3):
        t = m[d] * v[c] - bn * b[c]
        mom.append(t + total if c == d else t)
    flux = [m[d]] + mom + [(energy + total) * vn - bn * proj]
    flux += [vn * b[c] - v[c] * bn for c in others]
    a = G * p + bsq
    signal = jnp.abs(vn) + a * lax.rsqrt(a * rho)
    return cons, flux, signal


def face_flux(lower, upper, bn, d):
    def split(s):
        rest = list(s[5:])
        rest.insert(d, bn)
        return s[0], s[1:4], s[4], rest

    ul, fl, sl = wave(*split(lower), d)
    uu, fu, su = wave(*split(upper), d)
    signal = jnp.maximum(sl, su)
    return [0.5 * ((fl[n] + fu[n]) - signal * (uu[n] - ul[n])) for n in range(7)]


def along(prims, bn, d):
    low, high = (ylow, yhigh) if d == 1 else (zlow, zhigh)
    lower, upper = [], []
    for q in prims:
        diff = q - low(q)
        half = 0.5 * minmod(diff, high(diff))
        lower.append(low(q + half))
        upper.append(q - half)
    return face_flux(lower, upper, bn, d)


def rkl_factors():
    b = [1.0 / 3.0] * 3 + [
        (j * j + j - 2.0) / (2.0 * j * (j + 1.0)) for j in range(3, SUPER_SECTIONS + 1)
    ]
    w = 4.0 / (SUPER_SECTIONS * SUPER_SECTIONS + SUPER_SECTIONS - 2.0)
    rows = []
    for j in range(2, SECTIONS + 1):
        mu = (2.0 * j - 1.0) / j * b[j] / b[j - 1]
        nu = -(j - 1.0) / j * b[j] / b[j - 2]
        rate = mu * w * SUPER_TIME
        rows.append((mu, nu, 1.0 - mu - nu, rate, -(1.0 - b[j - 1]) * rate))
    return b[1] * w * SUPER_TIME, rows


def kernel(
    nx, ny,
    rho_ref, v_ref, p_ref, b_ref,
    rho_out, v_out, p_out, b_out,
    o_rho, o_v, o_p, o_b,
    ext, up, down, from_low, from_high,
    cell, fx_s, fy_s, fz_s, b_s,
    irho_s, kap_s, bc_s, bf_s, kx_s, ky_s, kz_s,
    t_s, r_s, pk, low_row, high_row,
    send_sem, recv_sem, in_sem, out_sem,
):
    cx, cy = o_rho.shape[0], o_rho.shape[1]
    gx, gy = lax.axis_index("gx"), lax.axis_index("gy")

    def target(dx, dy):
        return (lax.rem(gx + dx + nx, nx), lax.rem(gy + dy + ny, ny))

    ring = [(dx, dy) for dy in (1, -1, 0) for dx in (0, 1, -1) if (dx, dy) != (0, 0)]

    barrier = pltpu.get_barrier_semaphore()
    for dx, dy in ring:
        pl.semaphore_signal(barrier, inc=1, device_id=target(dx, dy), device_id_type=MESH)

    own, near = pl.ds(H, cx), pl.ds(0, cy)
    places = [
        (rho_ref, ext.at[0, own, near]),
        (v_ref, ext.at[pl.ds(1, 3), own, near]),
        (p_ref, ext.at[4, own, near]),
        (b_ref, ext.at[pl.ds(5, 3), own, near]),
    ]
    loads = [
        pltpu.make_async_copy(src, dst, in_sem.at[n]) for n, (src, dst) in enumerate(places)
    ]
    for load in loads:
        load.start()
    for load in loads:
        load.wait()
    for f in range(8):
        value = ext[f, H : H + cx, 0:cy, :]
        up[:, H * f : H * f + H, :] = value[:, cy - H : cy, :]
        down[:, H * f : H * f + H, :] = value[:, 0:H, :]
    pl.semaphore_wait(barrier, len(ring))

    def remote(phase, k, src, dst, to=None):
        copy = pltpu.make_async_remote_copy(
            src_ref=src,
            dst_ref=dst,
            send_sem=send_sem.at[phase, k],
            recv_sem=recv_sem.at[phase, k],
            device_id=target(*(to or ring[k])),
            device_id_type=MESH,
        )
        copy.start()
        return copy

    def side(k):
        return ring.index(k)

    wide = cx + 2 * H
    mine, low_h, high_h = pl.ds(H, cx), pl.ds(0, H), pl.ds(H + cx, H)
    first_h, last_h = pl.ds(H, H), pl.ds(cx, H)

    to_high = remote(0, side((0, 1)), up, from_low.at[mine])
    to_low = remote(0, side((0, -1)), down, from_high.at[mine])
    slabs = [
        remote(0, side((1, 0)), ext.at[:, last_h, near], ext.at[:, low_h, near]),
        remote(0, side((-1, 0)), ext.at[:, first_h, near], ext.at[:, high_h, near]),
    ]
    sent = [to_high, to_low] + slabs

    one = jnp.ones((ROWS, 128), jnp.float32)
    for n in range(3):
        b_s[n] = one

    A, B, BOTH = slice(0, cy), slice(cy, ROWS), slice(0, ROWS)

    def cells_own(s, e):
        bx, by, bz = (ext[5 + c, s:e, A] for c in range(3))
        nx_, nz_ = ext[5, s + 1 : e + 1, A], pltpu.roll(bz, 127, 2)
        cell[0, s:e, A] = 0.5 * (bx + nx_)
        cell[1, s:e, A] = by - 0.5 * ((nx_ - bx) + (nz_ - bz))
        cell[2, s:e, A] = 0.5 * (bz + nz_)

    def cell_x(s, e):
        cell[0, s:e, B] = 0.5 * (ext[5, s:e, B] + ext[5, s + 1 : e + 1, B])

    def cell_yz(s, e, rows):
        for x in range(s, e):
            by, bz = ext[6, x], ext[7, x, rows]
            cell[1, x, rows] = (0.5 * (by + yhigh(by)))[rows]
            cell[2, x, rows] = 0.5 * (bz + zhigh(bz))

    def prims(s, rows, d):
        return [ext[f, s, rows] for f in range(5)] + [
            cell[c, s, rows] for c in range(3) if c != d
        ]

    def flux_z(s, rows):
        for n, a in enumerate(along(prims(s, rows, 2), ext[7, s, rows], 2)):
            fz_s[n, s, rows] = a

    def flux_y(s):
        for n, a in enumerate(along(prims(s, BOTH, 1), ext[6, s], 1)):
            fy_s[n, s] = a

    def flux_x(i, rows):
        q = [prims(i + o, rows, 0) for o in (-2, -1, 0, 1)]
        lower, upper = [], []
        for q0, q1, q2, q3 in zip(*q):
            d1 = q2 - q1
            lower.append(q1 + 0.5 * minmod(q1 - q0, d1))
            upper.append(q2 - 0.5 * minmod(d1, q3 - q2))
        for n, a in enumerate(face_flux(lower, upper, ext[5, i, rows], 0)):
            fx_s[n, i, rows] = a

    def loop(count, f, unroll):
        def step(k, carry):
            f(k)
            return carry

        lax.fori_loop(0, count, step, 0, unroll=unroll)

    def outer(k):
        return k + 1 + (cx - 1) * ((k + cx - H) // (cx - 1))

    cells_own(H, H + cx - 1)
    loop(cx - 1, lambda k: flux_z(H + k, A), 1)
    for copy in slabs:
        copy.wait_recv()
    cells_own(0, H)
    cells_own(H + cx - 1, wide - 1)
    loop(cx - 1, lambda k: flux_z(outer(k), A), 1)
    loop(cx + 4, lambda k: flux_x(2 + k, A), 2)

    corners = []
    for copy, dy, buffer in ((to_high, 1, from_low), (to_low, -1, from_high)):
        copy.wait_recv()
        corners.append(remote(0, side((1, dy)), buffer.at[last_h], buffer.at[low_h], (1, 0)))
        corners.append(remote(0, side((-1, dy)), buffer.at[first_h], buffer.at[high_h], (-1, 0)))
    sent += corners

    def unpack(s, e):
        for f in range(8):
            ext[f, s:e, cy : cy + H, :] = from_high[s:e, H * f : H * f + H, :]
            ext[f, s:e, ROWS - H : ROWS, :] = from_low[s:e, H * f : H * f + H, :]

    unpack(H, H + cx)
    cell_x(H, H + cx - 1)
    cell_yz(H, H + cx, B)

    def middle(k):
        flux_y(H + k)
        flux_z(H + k, B)

    loop(cx - 1, middle, 1)
    loop(cx - 3, lambda k: flux_x(H + 2 + k, B), 1)

    for copy in corners:
        copy.wait_recv()
    unpack(0, H)
    unpack(H + cx, wide)
    cell_x(0, H)
    cell_x(H + cx - 1, wide - 1)
    cell_yz(0, H, B)
    cell_yz(H + cx, wide - 1, B)
    cell_yz(wide - 1, wide, BOTH)

    def ends(k):
        flux_y(outer(k))
        flux_z(outer(k), B)

    loop(cx - 1, ends, 1)
    loop(2 * H, lambda k: flux_x(2 + k + (cx - 3) * (k // H), B), 2)
    flux_x(wide - 2, A)

    def body(i):
        bx, by, bz = ext[5, i], ext[6, i], ext[7, i]
        xy, xz = fx_s[5, i], fx_s[6, i]
        yx, yz = fy_s[5, i], fy_s[6, i]
        zx, zy = fz_s[5, i], fz_s[6, i]
        ez = 0.25 * (fy_s[5, i - 1] + yx - ylow(xy) - xy)
        ey = 0.25 * (zlow(xz) + xz - fz_s[5, i - 1] - zx)
        ex = 0.25 * (ylow(zy) + zy - zlow(yz) - yz)
        bxn = bx - DT * (yhigh(ez) - ez) + DT * (zhigh(ey) - ey)
        bxo = b_s[0]
        byn = b_s[1] + DT * ez
        bzn = b_s[2] - DT * ey
        b_s[0] = bxn
        b_s[1] = by - DT * (zhigh(ex) - ex) - DT * ez
        b_s[2] = bz + DT * ey + DT * (yhigh(ex) - ex)

        m = i - 1
        rho, v, p = ext[0, m], [ext[1 + c, m] for c in range(3)], ext[4, m]
        bm = [cell[c, m] for c in range(3)]
        energy = (
            p * 1.5
            + 0.5 * rho * (v[0] * v[0] + v[1] * v[1] + v[2] * v[2])
            + 0.5 * (bm[0] * bm[0] + bm[1] * bm[1] + bm[2] * bm[2])
        )
        new = [rho, rho * v[0], rho * v[1], rho * v[2], energy]
        for n in range(5):
            fy, fz = fy_s[n, m], fz_s[n, m]
            change = (yhigh(fy) - fy) + (zhigh(fz) - fz) + (fx_s[n, i] - fx_s[n, m])
            new[n] = new[n] - DT * change

        floored = jnp.maximum(new[0], DENSITY_FLOOR)
        inv = 1.0 / floored
        vel = [new[1 + c] * inv for c in range(3)]
        bc = [0.5 * (bxo + bxn), 0.5 * (byn + yhigh(byn)), 0.5 * (bzn + zhigh(bzn))]
        kinetic = new[1] * vel[0] + new[2] * vel[1] + new[3] * vel[2]
        internal = new[4] - 0.5 * kinetic - 0.5 * (bc[0] * bc[0] + bc[1] * bc[1] + bc[2] * bc[2])
        p1 = jnp.maximum((G - 1.0) * internal, PRESSURE_FLOOR)
        t = p1 * inv
        irho_s[m] = (G - 1.0) * inv
        t_s[0, m] = t
        kap_s[m] = t * t * jnp.sqrt(t)
        for c in range(3):
            bc_s[c, m] = bc[c]
        for c, a in enumerate((bxo, byn, bzn)):
            bf_s[c, m] = a
        if isinstance(i, int):
            return
        x = jnp.maximum(m - H, 0)
        o_rho[x] = floored[A]
        for c in range(3):
            o_v[c, x] = vel[c][A]
        for c, a in enumerate((bxo, byn, bzn)):
            o_b[c, x] = a[A]

    body(2)
    loop(cx + 2, lambda k: body(3 + k), 2)
    body(wide - 3)
    body(wide - 2)
    stores = [
        pltpu.make_async_copy(src, dst, out_sem.at[n])
        for n, (src, dst) in enumerate(((o_rho, rho_out), (o_v, v_out), (o_b, b_out)))
    ]
    for store in stores:
        store.start()

    def coupling(s, carry):
        kap = kap_s[s]
        bc = [bc_s[c, s] for c in range(3)]
        bf = [bf_s[c, s] for c in range(3)]
        for d, out in enumerate((kx_s, ky_s, kz_s)):
            if d == 0:
                kl, bl = kap_s[s - 1], [bc_s[c, s - 1] for c in range(3)]
            else:
                low = ylow if d == 1 else zlow
                kl, bl = low(kap), [low(bc[c]) if c != d else None for c in range(3)]
            comp = [bf[d] if c == d else 0.5 * (bc[c] + bl[c]) for c in range(3)]
            mag = comp[0] * comp[0] + comp[1] * comp[1] + comp[2] * comp[2]
            factor = 0.5 * (kap + kl) / jnp.maximum(mag, FIELD_FLOOR) * bf[d]
            for c in range(3):
                out[c, s - H + 1] = factor * comp[c] * (1.0 if c == d else 0.25)
        return carry

    coupling(H - 1, 0)
    lax.fori_loop(H, H + cx + 2, coupling, 0, unroll=2)

    def rate(n, rim):
        rows = BOTH if rim else A
        t = {x: t_s[n, H + x] for x in range(-1 - rim, cx + 1 + rim)}
        dz = {x: zhigh(a) - zlow(a) for x, a in t.items()}
        dy = {x: (yhigh(a) - ylow(a))[rows] for x, a in t.items()}
        qx = {}
        for x in range(-rim, cx + 1 + rim):
            qx[x] = (
                kx_s[0, x + 1, rows] * (t[x] - t[x - 1])[rows]
                + kx_s[1, x + 1, rows] * (dy[x - 1] + dy[x])
                + kx_s[2, x + 1, rows] * (dz[x - 1] + dz[x])[rows]
            )
        out = []
        for x in range(-rim, cx + rim):
            a, dx, z = t[x], t[x + 1] - t[x - 1], dz[x]
            qy = (
                ky_s[1, x + 1] * (a - ylow(a))
                + ky_s[0, x + 1] * (dx + ylow(dx))
                + ky_s[2, x + 1] * (z + ylow(z))
            )
            a, dx, y = a[rows], dx[rows], dy[x]
            qz = (
                kz_s[2, x + 1, rows] * (a - zlow(a))
                + kz_s[0, x + 1, rows] * (dx + zlow(dx))
                + kz_s[1, x + 1, rows] * (y + zlow(y))
            )
            total = qx[x + 1] - qx[x] + (yhigh(qy) - qy)[rows] + (zhigh(qz) - qz)
            out.append(total * irho_s[H + x, rows])
        return jnp.stack(out)

    first_factor, factors = rkl_factors()
    inner, around = slice(H, H + cx), slice(H - 1, H + cx + 1)
    start = t_s[0, around]
    rate0 = rate(0, 1)
    r_s[...] = rate0
    t_s[1, around] = start + first_factor * rate0

    mu, nu, rest, fresh, zero = factors[0]
    second = (
        mu * t_s[1, inner, A]
        + (nu + rest) * t_s[0, inner, A]
        + zero * r_s[1 : cx + 1, A]
        + fresh * rate(1, 0)
    )
    for x in range(cx):
        for n in range(2):
            pk[0, n, x : x + 1, :] = second[x, cy - 2 + n : cy - 1 + n, :]
            pk[1, n, x : x + 1, :] = second[x, n : n + 1, :]
    t_s[2, inner, A] = second
    copies = []
    for k, (dx, dy) in enumerate(ring):
        if dy == 1:
            copies.append(remote(1, k, pk.at[0], low_row.at[dx + 1]))
        elif dy == -1:
            copies.append(remote(1, k, pk.at[1], high_row.at[dx + 1]))
        else:
            src = pl.ds(H + cx - 2 if dx == 1 else H, 2)
            dst = pl.ds(H - 2 if dx == 1 else H + cx, 2)
            copies.append(remote(1, k, t_s.at[2, src, near], t_s.at[2, dst, near]))
    mu, nu, rest, fresh, zero = factors[1]
    part = nu * t_s[1, around] + rest * t_s[0, around] + zero * r_s[...]
    for copy in copies:
        copy.wait_recv()
    sent += copies
    for x in range(-2, cx + 2):
        d = 2 if x < 0 else (0 if x >= cx else 1)
        row = x % cx
        for n in range(2):
            t_s[2, H + x, cy + n : cy + n + 1, :] = high_row[d, n, row : row + 1, :]
            t_s[2, H + x, ROWS - 2 + n : ROWS - 1 + n, :] = low_row[d, n, row : row + 1, :]
    t_s[3, around] = part + mu * t_s[2, around] + fresh * rate(2, 1)

    mu, nu, rest, fresh, zero = factors[2]
    last = (
        mu * t_s[3, inner, A]
        + nu * t_s[2, inner, A]
        + rest * t_s[0, inner, A]
        + zero * r_s[1 : cx + 1, A]
        + fresh * rate(3, 0)
    )
    o_p[...] = last * o_rho[...]
    stores.append(pltpu.make_async_copy(o_p, p_out, out_sem.at[3]))
    stores[3].start()
    for copy in sent:
        copy.wait_send()
    for store in stores:
        store.wait()


def hand_on(*refs):
    source, result, held, in_sem, out_sem = refs[:4], refs[4:8], refs[8:12], refs[12], refs[13]
    loads = [pltpu.make_async_copy(source[n], held[n], in_sem.at[n]) for n in range(4)]
    stores = [pltpu.make_async_copy(held[n], result[n], out_sem.at[n]) for n in range(4)]
    for load in loads:
        load.start()
    for load, store in zip(loads, stores):
        load.wait()
        store.start()
    for store in stores:
        store.wait()


def solution(mesh):
    nx, ny = mesh.shape["gx"], mesh.shape["gy"]

    def local(rho, v, p, b):
        cx, cy, nz = rho.shape
        wide = cx + 2 * H
        f32 = jnp.float32
        vm = lambda *shape: pltpu.VMEM(shape, f32)
        spec = pl.BlockSpec(memory_space=pl.ANY)
        shapes = [jax.ShapeDtypeStruct(a.shape, f32) for a in (rho, v, p, b)]
        results = pl.pallas_call(
            functools.partial(kernel, nx, ny),
            out_shape=shapes,
            in_specs=[pl.BlockSpec(memory_space=pltpu.HBM)] * 4,
            out_specs=[spec] * 4,
            scratch_shapes=[
                vm(cx, cy, nz),
                vm(3, cx, cy, nz),
                vm(cx, cy, nz),
                vm(3, cx, cy, nz),
                vm(8, wide, ROWS, nz),
                vm(cx, 8 * H, nz),
                vm(cx, 8 * H, nz),
                vm(wide, 8 * H, nz),
                vm(wide, 8 * H, nz),
                vm(3, wide, ROWS, nz),
                vm(7, wide, ROWS, nz),
                vm(7, wide, ROWS, nz),
                vm(7, wide, ROWS, nz),
                vm(3, ROWS, nz),
                vm(wide, ROWS, nz),
                vm(wide, ROWS, nz),
                vm(3, wide, ROWS, nz),
                vm(3, wide, ROWS, nz),
                vm(3, cx + 3, ROWS, nz),
                vm(3, cx + 3, ROWS, nz),
                vm(3, cx + 3, ROWS, nz),
                vm(SECTIONS, wide, ROWS, nz),
                vm(cx + 2, ROWS, nz),
                vm(2, 2, cx, nz),
                vm(3, 2, cx, nz),
                vm(3, 2, cx, nz),
                pltpu.SemaphoreType.DMA((2, 8)),
                pltpu.SemaphoreType.DMA((2, 8)),
                pltpu.SemaphoreType.DMA((4,)),
                pltpu.SemaphoreType.DMA((4,)),
            ],
            compiler_params=pltpu.CompilerParams(
                collective_id=0, has_side_effects=True, vmem_limit_bytes=16 << 20
            ),
        )(rho, v, p, b)
        return pl.pallas_call(
            hand_on,
            out_shape=shapes,
            in_specs=[spec] * 4,
            out_specs=[spec] * 4,
            scratch_shapes=[vm(*a.shape) for a in shapes]
            + [pltpu.SemaphoreType.DMA((4,)), pltpu.SemaphoreType.DMA((4,))],
            compiler_params=pltpu.CompilerParams(vmem_limit_bytes=16 << 20),
        )(*results)

    placed = (
        P("gx", "gy", None),
        P(None, "gx", "gy", None),
        P("gx", "gy", None),
        P(None, "gx", "gy", None),
    )
    return jax.shard_map(
        lambda *a: tuple(local(*a)),
        mesh=mesh,
        in_specs=placed,
        out_specs=placed,
        check_vma=False,
    )
```

```python
import functools

import jax
import jax.numpy as jnp
from jax import lax
from jax.experimental import pallas as pl
from jax.experimental.pallas import tpu as pltpu
from jax.sharding import PartitionSpec as P

SECTIONS = 4
SUPER_SECTIONS = 8

G = 5.0 / 3.0
DT = 0.04
SUPER_TIME = 0.08
DENSITY_FLOOR = 0.5
PRESSURE_FLOOR = 0.1
FIELD_FLOOR = 0.05

MESH = pl.DeviceIdType.MESH

H = 4
ROWS = 16


def ylow(a):
    return pltpu.roll(a, 1, 0)


def yhigh(a):
    return pltpu.roll(a, a.shape[0] - 1, 0)


def zlow(a):
    return pltpu.roll(a, 1, 1)


def zhigh(a):
    return pltpu.roll(a, a.shape[1] - 1, 1)


def minmod(a, b):
    return jnp.maximum(jnp.minimum(a, b), 0.0) + jnp.minimum(jnp.maximum(a, b), 0.0)


def wave(rho, v, p, b, d):
    bsq = b[0] * b[0] + b[1] * b[1] + b[2] * b[2]
    ksq = v[0] * v[0] + v[1] * v[1] + v[2] * v[2]
    half = 0.5 * bsq
    energy = p * 1.5 + 0.5 * rho * ksq + half
    total = p + half
    vn, bn = v[d], b[d]
    proj = v[0] * b[0] + v[1] * b[1] + v[2] * b[2]
    others = [c for c in range(3) if c != d]
    m = [rho * v[c] for c in range(3)]
    cons = [rho] + m + [energy] + [b[c] for c in others]
    mom = []
    for c in range(3):
        t = m[d] * v[c] - bn * b[c]
        mom.append(t + total if c == d else t)
    flux = [m[d]] + mom + [(energy + total) * vn - bn * proj]
    flux += [vn * b[c] - v[c] * bn for c in others]
    a = G * p + bsq
    signal = jnp.abs(vn) + a * lax.rsqrt(a * rho)
    return cons, flux, signal


def face_flux(lower, upper, bn, d):
    def split(s):
        rest = list(s[5:])
        rest.insert(d, bn)
        return s[0], s[1:4], s[4], rest

    ul, fl, sl = wave(*split(lower), d)
    uu, fu, su = wave(*split(upper), d)
    signal = jnp.maximum(sl, su)
    return [0.5 * ((fl[n] + fu[n]) - signal * (uu[n] - ul[n])) for n in range(7)]


def along(prims, bn, d):
    low, high = (ylow, yhigh) if d == 1 else (zlow, zhigh)
    lower, upper = [], []
    for q in prims:
        diff = q - low(q)
        half = 0.5 * minmod(diff, high(diff))
        lower.append(low(q + half))
        upper.append(q - half)
    return face_flux(lower, upper, bn, d)


def rkl_factors():
    b = [1.0 / 3.0] * 3 + [
        (j * j + j - 2.0) / (2.0 * j * (j + 1.0)) for j in range(3, SUPER_SECTIONS + 1)
    ]
    w = 4.0 / (SUPER_SECTIONS * SUPER_SECTIONS + SUPER_SECTIONS - 2.0)
    rows = []
    for j in range(2, SECTIONS + 1):
        mu = (2.0 * j - 1.0) / j * b[j] / b[j - 1]
        nu = -(j - 1.0) / j * b[j] / b[j - 2]
        rate = mu * w * SUPER_TIME
        rows.append((mu, nu, 1.0 - mu - nu, rate, -(1.0 - b[j - 1]) * rate))
    return b[1] * w * SUPER_TIME, rows


def kernel(
    nx, ny,
    rho_ref, v_ref, p_ref, b_ref,
    rho_out, v_out, p_out, b_out,
    o_rho, o_v, o_p, o_b,
    ext, up, down, from_low, from_high,
    cell, fx_s, fy_s, fz_s, b_s,
    irho_s, kap_s, bc_s, bf_s, kx_s, ky_s, kz_s,
    t_s, r_s, pk, low_row, high_row,
    send_sem, recv_sem, in_sem, out_sem,
):
    cx, cy = o_rho.shape[0], o_rho.shape[1]
    gx, gy = lax.axis_index("gx"), lax.axis_index("gy")

    def target(dx, dy):
        return (lax.rem(gx + dx + nx, nx), lax.rem(gy + dy + ny, ny))

    ring = [(dx, dy) for dy in (1, -1, 0) for dx in (0, 1, -1) if (dx, dy) != (0, 0)]

    barrier = pltpu.get_barrier_semaphore()
    for dx, dy in ring:
        pl.semaphore_signal(barrier, inc=1, device_id=target(dx, dy), device_id_type=MESH)

    own, near = pl.ds(H, cx), pl.ds(0, cy)
    places = [
        (rho_ref, ext.at[0, own, near]),
        (v_ref, ext.at[pl.ds(1, 3), own, near]),
        (p_ref, ext.at[4, own, near]),
        (b_ref, ext.at[pl.ds(5, 3), own, near]),
    ]
    loads = [
        pltpu.make_async_copy(src, dst, in_sem.at[n]) for n, (src, dst) in enumerate(places)
    ]
    for load in loads:
        load.start()
    for load in loads:
        load.wait()
    for f in range(8):
        value = ext[f, H : H + cx, 0:cy, :]
        up[:, H * f : H * f + H, :] = value[:, cy - H : cy, :]
        down[:, H * f : H * f + H, :] = value[:, 0:H, :]
    pl.semaphore_wait(barrier, len(ring))

    def remote(phase, k, src, dst, to=None):
        copy = pltpu.make_async_remote_copy(
            src_ref=src,
            dst_ref=dst,
            send_sem=send_sem.at[phase, k],
            recv_sem=recv_sem.at[phase, k],
            device_id=target(*(to or ring[k])),
            device_id_type=MESH,
        )
        copy.start()
        return copy

    def side(k):
        return ring.index(k)

    wide = cx + 2 * H
    mine, low_h, high_h = pl.ds(H, cx), pl.ds(0, H), pl.ds(H + cx, H)
    first_h, last_h = pl.ds(H, H), pl.ds(cx, H)

    to_high = remote(0, side((0, 1)), up, from_low.at[mine])
    to_low = remote(0, side((0, -1)), down, from_high.at[mine])
    slabs = [
        remote(0, side((1, 0)), ext.at[:, last_h, near], ext.at[:, low_h, near]),
        remote(0, side((-1, 0)), ext.at[:, first_h, near], ext.at[:, high_h, near]),
    ]
    sent = [to_high, to_low] + slabs

    one = jnp.ones((ROWS, 128), jnp.float32)
    for n in range(3):
        b_s[n] = one

    A, B, BOTH = slice(0, cy), slice(cy, ROWS), slice(0, ROWS)

    def cells_own(s, e):
        bx, by, bz = (ext[5 + c, s:e, A] for c in range(3))
        nx_, nz_ = ext[5, s + 1 : e + 1, A], pltpu.roll(bz, 127, 2)
        cell[0, s:e, A] = 0.5 * (bx + nx_)
        cell[1, s:e, A] = by - 0.5 * ((nx_ - bx) + (nz_ - bz))
        cell[2, s:e, A] = 0.5 * (bz + nz_)

    def cell_x(s, e):
        cell[0, s:e, B] = 0.5 * (ext[5, s:e, B] + ext[5, s + 1 : e + 1, B])

    def cell_yz(s, e, rows):
        for x in range(s, e):
            by, bz = ext[6, x], ext[7, x, rows]
            cell[1, x, rows] = (0.5 * (by + yhigh(by)))[rows]
            cell[2, x, rows] = 0.5 * (bz + zhigh(bz))

    def prims(s, rows, d):
        return [ext[f, s, rows] for f in range(5)] + [
            cell[c, s, rows] for c in range(3) if c != d
        ]

    def flux_z(s, rows):
        for n, a in enumerate(along(prims(s, rows, 2), ext[7, s, rows], 2)):
            fz_s[n, s, rows] = a

    def flux_y(s):
        for n, a in enumerate(along(prims(s, BOTH, 1), ext[6, s], 1)):
            fy_s[n, s] = a

    def flux_x(i, rows):
        q = [prims(i + o, rows, 0) for o in (-2, -1, 0, 1)]
        lower, upper = [], []
        for q0, q1, q2, q3 in zip(*q):
            d1 = q2 - q1
            lower.append(q1 + 0.5 * minmod(q1 - q0, d1))
            upper.append(q2 - 0.5 * minmod(d1, q3 - q2))
        for n, a in enumerate(face_flux(lower, upper, ext[5, i, rows], 0)):
            fx_s[n, i, rows] = a

    def loop(count, f, unroll):
        def step(k, carry):
            f(k)
            return carry

        lax.fori_loop(0, count, step, 0, unroll=unroll)

    def outer(k):
        return k + 1 + (cx - 1) * ((k + cx - H) // (cx - 1))

    cells_own(H, H + cx - 1)
    loop(cx - 1, lambda k: flux_z(H + k, A), cx - 1)
    for copy in slabs:
        copy.wait_recv()
    cells_own(0, H)
    cells_own(H + cx - 1, wide - 1)
    loop(cx - 1, lambda k: flux_z(outer(k), A), cx - 1)
    loop(cx + 4, lambda k: flux_x(2 + k, A), 4)

    corners = []
    for copy, dy, buffer in ((to_high, 1, from_low), (to_low, -1, from_high)):
        copy.wait_recv()
        corners.append(remote(0, side((1, dy)), buffer.at[last_h], buffer.at[low_h], (1, 0)))
        corners.append(remote(0, side((-1, dy)), buffer.at[first_h], buffer.at[high_h], (-1, 0)))
    sent += corners

    def unpack(s, e):
        for f in range(8):
            ext[f, s:e, cy : cy + H, :] = from_high[s:e, H * f : H * f + H, :]
            ext[f, s:e, ROWS - H : ROWS, :] = from_low[s:e, H * f : H * f + H, :]

    unpack(H, H + cx)
    cell_x(H, H + cx - 1)
    cell_yz(H, H + cx, B)

    def middle(k):
        flux_y(H + k)
        flux_z(H + k, B)

    loop(cx - 1, middle, cx - 1)
    loop(cx - 3, lambda k: flux_x(H + 2 + k, B), cx - 3)

    for copy in corners:
        copy.wait_recv()
    unpack(0, H)
    unpack(H + cx, wide)
    cell_x(0, H)
    cell_x(H + cx - 1, wide - 1)
    cell_yz(0, H, B)
    cell_yz(H + cx, wide - 1, B)
    cell_yz(wide - 1, wide, BOTH)

    def ends(k):
        flux_y(outer(k))
        flux_z(outer(k), B)

    loop(cx - 1, ends, cx - 1)
    loop(2 * H, lambda k: flux_x(2 + k + (cx - 3) * (k // H), B), H)
    flux_x(wide - 2, A)

    def body(i):
        bx, by, bz = ext[5, i], ext[6, i], ext[7, i]
        xy, xz = fx_s[5, i], fx_s[6, i]
        yx, yz = fy_s[5, i], fy_s[6, i]
        zx, zy = fz_s[5, i], fz_s[6, i]
        ez = 0.25 * (fy_s[5, i - 1] + yx - ylow(xy) - xy)
        ey = 0.25 * (zlow(xz) + xz - fz_s[5, i - 1] - zx)
        ex = 0.25 * (ylow(zy) + zy - zlow(yz) - yz)
        bxn = bx - DT * (yhigh(ez) - ez) + DT * (zhigh(ey) - ey)
        bxo = b_s[0]
        byn = b_s[1] + DT * ez
        bzn = b_s[2] - DT * ey
        b_s[0] = bxn
        b_s[1] = by - DT * (zhigh(ex) - ex) - DT * ez
        b_s[2] = bz + DT * ey + DT * (yhigh(ex) - ex)

        m = i - 1
        rho, v, p = ext[0, m], [ext[1 + c, m] for c in range(3)], ext[4, m]
        bm = [cell[c, m] for c in range(3)]
        energy = (
            p * 1.5
            + 0.5 * rho * (v[0] * v[0] + v[1] * v[1] + v[2] * v[2])
            + 0.5 * (bm[0] * bm[0] + bm[1] * bm[1] + bm[2] * bm[2])
        )
        new = [rho, rho * v[0], rho * v[1], rho * v[2], energy]
        for n in range(5):
            fy, fz = fy_s[n, m], fz_s[n, m]
            change = (yhigh(fy) - fy) + (zhigh(fz) - fz) + (fx_s[n, i] - fx_s[n, m])
            new[n] = new[n] - DT * change

        floored = jnp.maximum(new[0], DENSITY_FLOOR)
        inv = 1.0 / floored
        vel = [new[1 + c] * inv for c in range(3)]
        bc = [0.5 * (bxo + bxn), 0.5 * (byn + yhigh(byn)), 0.5 * (bzn + zhigh(bzn))]
        kinetic = new[1] * vel[0] + new[2] * vel[1] + new[3] * vel[2]
        internal = new[4] - 0.5 * kinetic - 0.5 * (bc[0] * bc[0] + bc[1] * bc[1] + bc[2] * bc[2])
        p1 = jnp.maximum((G - 1.0) * internal, PRESSURE_FLOOR)
        t = p1 * inv
        irho_s[m] = (G - 1.0) * inv
        t_s[0, m] = t
        kap_s[m] = t * t * jnp.sqrt(t)
        for c in range(3):
            bc_s[c, m] = bc[c]
        for c, a in enumerate((bxo, byn, bzn)):
            bf_s[c, m] = a
        if isinstance(i, int):
            return
        x = jnp.maximum(m - H, 0)
        o_rho[x] = floored[A]
        for c in range(3):
            o_v[c, x] = vel[c][A]
        for c, a in enumerate((bxo, byn, bzn)):
            o_b[c, x] = a[A]

    body(2)
    loop(cx + 2, lambda k: body(3 + k), 5)
    body(wide - 3)
    body(wide - 2)
    stores = [
        pltpu.make_async_copy(src, dst, out_sem.at[n])
        for n, (src, dst) in enumerate(((o_rho, rho_out), (o_v, v_out), (o_b, b_out)))
    ]
    for store in stores:
        store.start()

    def coupling(s, carry):
        kap = kap_s[s]
        bc = [bc_s[c, s] for c in range(3)]
        bf = [bf_s[c, s] for c in range(3)]
        for d, out in enumerate((kx_s, ky_s, kz_s)):
            if d == 0:
                kl, bl = kap_s[s - 1], [bc_s[c, s - 1] for c in range(3)]
            else:
                low = ylow if d == 1 else zlow
                kl, bl = low(kap), [low(bc[c]) if c != d else None for c in range(3)]
            comp = [bf[d] if c == d else 0.5 * (bc[c] + bl[c]) for c in range(3)]
            mag = comp[0] * comp[0] + comp[1] * comp[1] + comp[2] * comp[2]
            factor = 0.5 * (kap + kl) / jnp.maximum(mag, FIELD_FLOOR) * bf[d]
            for c in range(3):
                out[c, s - H + 1] = factor * comp[c] * (1.0 if c == d else 0.25)
        return carry

    coupling(H - 1, 0)
    lax.fori_loop(H, H + cx + 2, coupling, 0, unroll=5)

    def rate(n, rim):
        rows = BOTH if rim else A
        t = {x: t_s[n, H + x] for x in range(-1 - rim, cx + 1 + rim)}
        dz = {x: zhigh(a) - zlow(a) for x, a in t.items()}
        dy = {x: (yhigh(a) - ylow(a))[rows] for x, a in t.items()}
        qx = {}
        for x in range(-rim, cx + 1 + rim):
            qx[x] = (
                kx_s[0, x + 1, rows] * (t[x] - t[x - 1])[rows]
                + kx_s[1, x + 1, rows] * (dy[x - 1] + dy[x])
                + kx_s[2, x + 1, rows] * (dz[x - 1] + dz[x])[rows]
            )
        out = []
        for x in range(-rim, cx + rim):
            a, dx, z = t[x], t[x + 1] - t[x - 1], dz[x]
            qy = (
                ky_s[1, x + 1] * (a - ylow(a))
                + ky_s[0, x + 1] * (dx + ylow(dx))
                + ky_s[2, x + 1] * (z + ylow(z))
            )
            a, dx, y = a[rows], dx[rows], dy[x]
            qz = (
                kz_s[2, x + 1, rows] * (a - zlow(a))
                + kz_s[0, x + 1, rows] * (dx + zlow(dx))
                + kz_s[1, x + 1, rows] * (y + zlow(y))
            )
            total = qx[x + 1] - qx[x] + (yhigh(qy) - qy)[rows] + (zhigh(qz) - qz)
            out.append(total * irho_s[H + x, rows])
        return jnp.stack(out)

    first_factor, factors = rkl_factors()
    inner, around = slice(H, H + cx), slice(H - 1, H + cx + 1)
    start = t_s[0, around]
    rate0 = rate(0, 1)
    r_s[...] = rate0
    t_s[1, around] = start + first_factor * rate0

    mu, nu, rest, fresh, zero = factors[0]
    second = (
        mu * t_s[1, inner, A]
        + (nu + rest) * t_s[0, inner, A]
        + zero * r_s[1 : cx + 1, A]
        + fresh * rate(1, 0)
    )
    for x in range(cx):
        for n in range(2):
            pk[0, n, x : x + 1, :] = second[x, cy - 2 + n : cy - 1 + n, :]
            pk[1, n, x : x + 1, :] = second[x, n : n + 1, :]
    t_s[2, inner, A] = second
    copies = []
    for k, (dx, dy) in enumerate(ring):
        if dy == 1:
            copies.append(remote(1, k, pk.at[0], low_row.at[dx + 1]))
        elif dy == -1:
            copies.append(remote(1, k, pk.at[1], high_row.at[dx + 1]))
        else:
            src = pl.ds(H + cx - 2 if dx == 1 else H, 2)
            dst = pl.ds(H - 2 if dx == 1 else H + cx, 2)
            copies.append(remote(1, k, t_s.at[2, src, near], t_s.at[2, dst, near]))
    mu, nu, rest, fresh, zero = factors[1]
    part = nu * t_s[1, around] + rest * t_s[0, around] + zero * r_s[...]
    for copy in copies:
        copy.wait_recv()
    sent += copies
    for x in range(-2, cx + 2):
        d = 2 if x < 0 else (0 if x >= cx else 1)
        row = x % cx
        for n in range(2):
            t_s[2, H + x, cy + n : cy + n + 1, :] = high_row[d, n, row : row + 1, :]
            t_s[2, H + x, ROWS - 2 + n : ROWS - 1 + n, :] = low_row[d, n, row : row + 1, :]
    t_s[3, around] = part + mu * t_s[2, around] + fresh * rate(2, 1)

    mu, nu, rest, fresh, zero = factors[2]
    last = (
        mu * t_s[3, inner, A]
        + nu * t_s[2, inner, A]
        + rest * t_s[0, inner, A]
        + zero * r_s[1 : cx + 1, A]
        + fresh * rate(3, 0)
    )
    o_p[...] = last * o_rho[...]
    stores.append(pltpu.make_async_copy(o_p, p_out, out_sem.at[3]))
    stores[3].start()
    for copy in sent:
        copy.wait_send()
    for store in stores:
        store.wait()


def hand_on(*refs):
    source, result, held, in_sem, out_sem = refs[:4], refs[4:8], refs[8:12], refs[12], refs[13]
    loads = [pltpu.make_async_copy(source[n], held[n], in_sem.at[n]) for n in range(4)]
    stores = [pltpu.make_async_copy(held[n], result[n], out_sem.at[n]) for n in range(4)]
    for load in loads:
        load.start()
    for load, store in zip(loads, stores):
        load.wait()
        store.start()
    for store in stores:
        store.wait()


def solution(mesh):
    nx, ny = mesh.shape["gx"], mesh.shape["gy"]

    def local(rho, v, p, b):
        cx, cy, nz = rho.shape
        wide = cx + 2 * H
        f32 = jnp.float32
        vm = lambda *shape: pltpu.VMEM(shape, f32)
        spec = pl.BlockSpec(memory_space=pl.ANY)
        shapes = [jax.ShapeDtypeStruct(a.shape, f32) for a in (rho, v, p, b)]
        results = pl.pallas_call(
            functools.partial(kernel, nx, ny),
            out_shape=shapes,
            in_specs=[pl.BlockSpec(memory_space=pltpu.HBM)] * 4,
            out_specs=[spec] * 4,
            scratch_shapes=[
                vm(cx, cy, nz),
                vm(3, cx, cy, nz),
                vm(cx, cy, nz),
                vm(3, cx, cy, nz),
                vm(8, wide, ROWS, nz),
                vm(cx, 8 * H, nz),
                vm(cx, 8 * H, nz),
                vm(wide, 8 * H, nz),
                vm(wide, 8 * H, nz),
                vm(3, wide, ROWS, nz),
                vm(7, wide, ROWS, nz),
                vm(7, wide, ROWS, nz),
                vm(7, wide, ROWS, nz),
                vm(3, ROWS, nz),
                vm(wide, ROWS, nz),
                vm(wide, ROWS, nz),
                vm(3, wide, ROWS, nz),
                vm(3, wide, ROWS, nz),
                vm(3, cx + 3, ROWS, nz),
                vm(3, cx + 3, ROWS, nz),
                vm(3, cx + 3, ROWS, nz),
                vm(SECTIONS, wide, ROWS, nz),
                vm(cx + 2, ROWS, nz),
                vm(2, 2, cx, nz),
                vm(3, 2, cx, nz),
                vm(3, 2, cx, nz),
                pltpu.SemaphoreType.DMA((2, 8)),
                pltpu.SemaphoreType.DMA((2, 8)),
                pltpu.SemaphoreType.DMA((4,)),
                pltpu.SemaphoreType.DMA((4,)),
            ],
            compiler_params=pltpu.CompilerParams(collective_id=0, has_side_effects=True),
        )(rho, v, p, b)
        return pl.pallas_call(
            hand_on,
            out_shape=shapes,
            in_specs=[spec] * 4,
            out_specs=[spec] * 4,
            scratch_shapes=[vm(*a.shape) for a in shapes]
            + [pltpu.SemaphoreType.DMA((4,)), pltpu.SemaphoreType.DMA((4,))],
        )(*results)

    placed = (
        P("gx", "gy", None),
        P(None, "gx", "gy", None),
        P("gx", "gy", None),
        P(None, "gx", "gy", None),
    )
    return jax.shard_map(
        lambda *a: tuple(local(*a)),
        mesh=mesh,
        in_specs=placed,
        out_specs=placed,
        check_vma=False,
    )
```

```python
import functools

import jax
import jax.numpy as jnp
from jax import lax
from jax.experimental import pallas as pl
from jax.experimental.pallas import tpu as pltpu
from jax.sharding import PartitionSpec as P

SECTIONS = 4
SUPER_SECTIONS = 8

G = 5.0 / 3.0
DT = 0.04
SUPER_TIME = 0.08
DENSITY_FLOOR = 0.5
PRESSURE_FLOOR = 0.1
FIELD_FLOOR = 0.05

MESH = pl.DeviceIdType.MESH

H = 4
ROWS = 16


def ylow(a):
    return pltpu.roll(a, 1, 0)


def yhigh(a):
    return pltpu.roll(a, a.shape[0] - 1, 0)


def zlow(a):
    return pltpu.roll(a, 1, 1)


def zhigh(a):
    return pltpu.roll(a, a.shape[1] - 1, 1)


def minmod(a, b):
    return jnp.maximum(jnp.minimum(a, b), 0.0) + jnp.minimum(jnp.maximum(a, b), 0.0)


def wave(rho, v, p, b, d):
    bsq = b[0] * b[0] + b[1] * b[1] + b[2] * b[2]
    ksq = v[0] * v[0] + v[1] * v[1] + v[2] * v[2]
    half = 0.5 * bsq
    energy = p * 1.5 + 0.5 * rho * ksq + half
    total = p + half
    vn, bn = v[d], b[d]
    proj = v[0] * b[0] + v[1] * b[1] + v[2] * b[2]
    others = [c for c in range(3) if c != d]
    m = [rho * v[c] for c in range(3)]
    cons = [rho] + m + [energy] + [b[c] for c in others]
    mom = []
    for c in range(3):
        t = m[d] * v[c] - bn * b[c]
        mom.append(t + total if c == d else t)
    flux = [m[d]] + mom + [(energy + total) * vn - bn * proj]
    flux += [vn * b[c] - v[c] * bn for c in others]
    a = G * p + bsq
    signal = jnp.abs(vn) + a * lax.rsqrt(a * rho)
    return cons, flux, signal


def face_flux(lower, upper, bn, d):
    def split(s):
        rest = list(s[5:])
        rest.insert(d, bn)
        return s[0], s[1:4], s[4], rest

    ul, fl, sl = wave(*split(lower), d)
    uu, fu, su = wave(*split(upper), d)
    signal = jnp.maximum(sl, su)
    return [0.5 * ((fl[n] + fu[n]) - signal * (uu[n] - ul[n])) for n in range(7)]


def along(prims, bn, d):
    low, high = (ylow, yhigh) if d == 1 else (zlow, zhigh)
    lower, upper = [], []
    for q in prims:
        diff = q - low(q)
        half = 0.5 * minmod(diff, high(diff))
        lower.append(low(q + half))
        upper.append(q - half)
    return face_flux(lower, upper, bn, d)


def rkl_factors():
    b = [1.0 / 3.0] * 3 + [
        (j * j + j - 2.0) / (2.0 * j * (j + 1.0)) for j in range(3, SUPER_SECTIONS + 1)
    ]
    w = 4.0 / (SUPER_SECTIONS * SUPER_SECTIONS + SUPER_SECTIONS - 2.0)
    rows = []
    for j in range(2, SECTIONS + 1):
        mu = (2.0 * j - 1.0) / j * b[j] / b[j - 1]
        nu = -(j - 1.0) / j * b[j] / b[j - 2]
        rate = mu * w * SUPER_TIME
        rows.append((mu, nu, 1.0 - mu - nu, rate, -(1.0 - b[j - 1]) * rate))
    return b[1] * w * SUPER_TIME, rows


def kernel(
    nx, ny,
    rho_ref, v_ref, p_ref, b_ref,
    rho_out, v_out, p_out, b_out,
    o_rho, o_v, o_p, o_b,
    ext, up, down, from_low, from_high,
    cell, fx_s, fy_s, fz_s, b_s,
    irho_s, kap_s, bc_s, bf_s, kx_s, ky_s, kz_s,
    t_s, r_s, pk, low_row, high_row,
    send_sem, recv_sem, in_sem, out_sem,
):
    cx, cy = o_rho.shape[0], o_rho.shape[1]
    gx, gy = lax.axis_index("gx"), lax.axis_index("gy")

    def target(dx, dy):
        return (lax.rem(gx + dx + nx, nx), lax.rem(gy + dy + ny, ny))

    ring = [(dx, dy) for dy in (1, -1, 0) for dx in (0, 1, -1) if (dx, dy) != (0, 0)]

    barrier = pltpu.get_barrier_semaphore()
    for dx, dy in ring:
        pl.semaphore_signal(barrier, inc=1, device_id=target(dx, dy), device_id_type=MESH)

    own, near = pl.ds(H, cx), pl.ds(0, cy)
    places = [
        (rho_ref, ext.at[0, own, near]),
        (v_ref, ext.at[pl.ds(1, 3), own, near]),
        (p_ref, ext.at[4, own, near]),
        (b_ref, ext.at[pl.ds(5, 3), own, near]),
    ]
    loads = [
        pltpu.make_async_copy(src, dst, in_sem.at[n]) for n, (src, dst) in enumerate(places)
    ]
    for load in loads:
        load.start()
    for load in loads:
        load.wait()
    for f in range(8):
        value = ext[f, H : H + cx, 0:cy, :]
        up[:, H * f : H * f + H, :] = value[:, cy - H : cy, :]
        down[:, H * f : H * f + H, :] = value[:, 0:H, :]
    pl.semaphore_wait(barrier, len(ring))

    def remote(phase, k, src, dst, to=None):
        copy = pltpu.make_async_remote_copy(
            src_ref=src,
            dst_ref=dst,
            send_sem=send_sem.at[phase, k],
            recv_sem=recv_sem.at[phase, k],
            device_id=target(*(to or ring[k])),
            device_id_type=MESH,
        )
        copy.start()
        return copy

    def side(k):
        return ring.index(k)

    wide = cx + 2 * H
    mine, low_h, high_h = pl.ds(H, cx), pl.ds(0, H), pl.ds(H + cx, H)
    first_h, last_h = pl.ds(H, H), pl.ds(cx, H)

    to_high = remote(0, side((0, 1)), up, from_low.at[mine])
    to_low = remote(0, side((0, -1)), down, from_high.at[mine])
    slabs = [
        remote(0, side((1, 0)), ext.at[:, last_h, near], ext.at[:, low_h, near]),
        remote(0, side((-1, 0)), ext.at[:, first_h, near], ext.at[:, high_h, near]),
    ]
    sent = [to_high, to_low] + slabs

    one = jnp.ones((ROWS, 128), jnp.float32)
    for n in range(3):
        b_s[n] = one

    A, B, BOTH = slice(0, cy), slice(cy, ROWS), slice(0, ROWS)

    def cells_own(s, e):
        bx, by, bz = (ext[5 + c, s:e, A] for c in range(3))
        nx_, nz_ = ext[5, s + 1 : e + 1, A], pltpu.roll(bz, 127, 2)
        cell[0, s:e, A] = 0.5 * (bx + nx_)
        cell[1, s:e, A] = by - 0.5 * ((nx_ - bx) + (nz_ - bz))
        cell[2, s:e, A] = 0.5 * (bz + nz_)

    def cell_x(s, e):
        cell[0, s:e, B] = 0.5 * (ext[5, s:e, B] + ext[5, s + 1 : e + 1, B])

    def cell_yz(s, e, rows):
        for x in range(s, e):
            by, bz = ext[6, x], ext[7, x, rows]
            cell[1, x, rows] = (0.5 * (by + yhigh(by)))[rows]
            cell[2, x, rows] = 0.5 * (bz + zhigh(bz))

    def prims(s, rows, d):
        return [ext[f, s, rows] for f in range(5)] + [
            cell[c, s, rows] for c in range(3) if c != d
        ]

    def flux_z(s, rows):
        for n, a in enumerate(along(prims(s, rows, 2), ext[7, s, rows], 2)):
            fz_s[n, s, rows] = a

    def flux_y(s):
        for n, a in enumerate(along(prims(s, BOTH, 1), ext[6, s], 1)):
            fy_s[n, s] = a

    def flux_x(i, rows):
        q = [prims(i + o, rows, 0) for o in (-2, -1, 0, 1)]
        lower, upper = [], []
        for q0, q1, q2, q3 in zip(*q):
            d1 = q2 - q1
            lower.append(q1 + 0.5 * minmod(q1 - q0, d1))
            upper.append(q2 - 0.5 * minmod(d1, q3 - q2))
        for n, a in enumerate(face_flux(lower, upper, ext[5, i, rows], 0)):
            fx_s[n, i, rows] = a

    def loop(count, f, unroll):
        def step(k, carry):
            f(k)
            return carry

        lax.fori_loop(0, count, step, 0, unroll=unroll)

    def outer(k):
        return k + 1 + (cx - 1) * ((k + cx - H) // (cx - 1))

    cells_own(H, H + cx - 1)
    loop(cx - 1, lambda k: flux_z(H + k, A), cx - 1)
    for copy in slabs:
        copy.wait_recv()
    cells_own(0, H)
    cells_own(H + cx - 1, wide - 1)
    loop(cx - 1, lambda k: flux_z(outer(k), A), cx - 1)
    loop(cx + 4, lambda k: flux_x(2 + k, A), 6)

    corners = []
    for copy, dy, buffer in ((to_high, 1, from_low), (to_low, -1, from_high)):
        copy.wait_recv()
        corners.append(remote(0, side((1, dy)), buffer.at[last_h], buffer.at[low_h], (1, 0)))
        corners.append(remote(0, side((-1, dy)), buffer.at[first_h], buffer.at[high_h], (-1, 0)))
    sent += corners

    def unpack(s, e):
        for f in range(8):
            ext[f, s:e, cy : cy + H, :] = from_high[s:e, H * f : H * f + H, :]
            ext[f, s:e, ROWS - H : ROWS, :] = from_low[s:e, H * f : H * f + H, :]

    unpack(H, H + cx)
    cell_x(H, H + cx - 1)
    cell_yz(H, H + cx, B)

    def middle(k):
        flux_y(H + k)
        flux_z(H + k, B)

    loop(cx - 1, middle, cx - 1)
    loop(cx - 3, lambda k: flux_x(H + 2 + k, B), cx - 3)

    for copy in corners:
        copy.wait_recv()
    unpack(0, H)
    unpack(H + cx, wide)
    cell_x(0, H)
    cell_x(H + cx - 1, wide - 1)
    cell_yz(0, H, B)
    cell_yz(H + cx, wide - 1, B)
    cell_yz(wide - 1, wide, BOTH)

    def ends(k):
        flux_y(outer(k))
        flux_z(outer(k), B)

    loop(cx - 1, ends, cx - 1)
    loop(2 * H, lambda k: flux_x(2 + k + (cx - 3) * (k // H), B), 2 * H)
    flux_x(wide - 2, A)

    def body(i):
        bx, by, bz = ext[5, i], ext[6, i], ext[7, i]
        xy, xz = fx_s[5, i], fx_s[6, i]
        yx, yz = fy_s[5, i], fy_s[6, i]
        zx, zy = fz_s[5, i], fz_s[6, i]
        ez = 0.25 * (fy_s[5, i - 1] + yx - ylow(xy) - xy)
        ey = 0.25 * (zlow(xz) + xz - fz_s[5, i - 1] - zx)
        ex = 0.25 * (ylow(zy) + zy - zlow(yz) - yz)
        bxn = bx - DT * (yhigh(ez) - ez) + DT * (zhigh(ey) - ey)
        bxo = b_s[0]
        byn = b_s[1] + DT * ez
        bzn = b_s[2] - DT * ey
        b_s[0] = bxn
        b_s[1] = by - DT * (zhigh(ex) - ex) - DT * ez
        b_s[2] = bz + DT * ey + DT * (yhigh(ex) - ex)

        m = i - 1
        rho, v, p = ext[0, m], [ext[1 + c, m] for c in range(3)], ext[4, m]
        bm = [cell[c, m] for c in range(3)]
        energy = (
            p * 1.5
            + 0.5 * rho * (v[0] * v[0] + v[1] * v[1] + v[2] * v[2])
            + 0.5 * (bm[0] * bm[0] + bm[1] * bm[1] + bm[2] * bm[2])
        )
        new = [rho, rho * v[0], rho * v[1], rho * v[2], energy]
        for n in range(5):
            fy, fz = fy_s[n, m], fz_s[n, m]
            change = (yhigh(fy) - fy) + (zhigh(fz) - fz) + (fx_s[n, i] - fx_s[n, m])
            new[n] = new[n] - DT * change

        floored = jnp.maximum(new[0], DENSITY_FLOOR)
        inv = 1.0 / floored
        vel = [new[1 + c] * inv for c in range(3)]
        bc = [0.5 * (bxo + bxn), 0.5 * (byn + yhigh(byn)), 0.5 * (bzn + zhigh(bzn))]
        kinetic = new[1] * vel[0] + new[2] * vel[1] + new[3] * vel[2]
        internal = new[4] - 0.5 * kinetic - 0.5 * (bc[0] * bc[0] + bc[1] * bc[1] + bc[2] * bc[2])
        p1 = jnp.maximum((G - 1.0) * internal, PRESSURE_FLOOR)
        t = p1 * inv
        irho_s[m] = (G - 1.0) * inv
        t_s[0, m] = t
        kap_s[m] = t * t * jnp.sqrt(t)
        for c in range(3):
            bc_s[c, m] = bc[c]
        for c, a in enumerate((bxo, byn, bzn)):
            bf_s[c, m] = a
        if isinstance(i, int):
            return
        x = jnp.maximum(m - H, 0)
        o_rho[x] = floored[A]
        for c in range(3):
            o_v[c, x] = vel[c][A]
        for c, a in enumerate((bxo, byn, bzn)):
            o_b[c, x] = a[A]

    body(2)
    loop(cx + 2, lambda k: body(3 + k), 10)
    body(wide - 3)
    body(wide - 2)
    stores = [
        pltpu.make_async_copy(src, dst, out_sem.at[n])
        for n, (src, dst) in enumerate(((o_rho, rho_out), (o_v, v_out), (o_b, b_out)))
    ]
    for store in stores:
        store.start()

    def coupling(s, carry):
        kap = kap_s[s]
        bc = [bc_s[c, s] for c in range(3)]
        bf = [bf_s[c, s] for c in range(3)]
        for d, out in enumerate((kx_s, ky_s, kz_s)):
            if d == 0:
                kl, bl = kap_s[s - 1], [bc_s[c, s - 1] for c in range(3)]
            else:
                low = ylow if d == 1 else zlow
                kl, bl = low(kap), [low(bc[c]) if c != d else None for c in range(3)]
            comp = [bf[d] if c == d else 0.5 * (bc[c] + bl[c]) for c in range(3)]
            mag = comp[0] * comp[0] + comp[1] * comp[1] + comp[2] * comp[2]
            factor = 0.5 * (kap + kl) / jnp.maximum(mag, FIELD_FLOOR) * bf[d]
            for c in range(3):
                out[c, s - H + 1] = factor * comp[c] * (1.0 if c == d else 0.25)
        return carry

    coupling(H - 1, 0)
    lax.fori_loop(H, H + cx + 2, coupling, 0, unroll=10)

    def rate(n, rim):
        rows = BOTH if rim else A
        t = {x: t_s[n, H + x] for x in range(-1 - rim, cx + 1 + rim)}
        dz = {x: zhigh(a) - zlow(a) for x, a in t.items()}
        dy = {x: (yhigh(a) - ylow(a))[rows] for x, a in t.items()}
        qx = {}
        for x in range(-rim, cx + 1 + rim):
            qx[x] = (
                kx_s[0, x + 1, rows] * (t[x] - t[x - 1])[rows]
                + kx_s[1, x + 1, rows] * (dy[x - 1] + dy[x])
                + kx_s[2, x + 1, rows] * (dz[x - 1] + dz[x])[rows]
            )
        out = []
        for x in range(-rim, cx + rim):
            a, dx, z = t[x], t[x + 1] - t[x - 1], dz[x]
            qy = (
                ky_s[1, x + 1] * (a - ylow(a))
                + ky_s[0, x + 1] * (dx + ylow(dx))
                + ky_s[2, x + 1] * (z + ylow(z))
            )
            a, dx, y = a[rows], dx[rows], dy[x]
            qz = (
                kz_s[2, x + 1, rows] * (a - zlow(a))
                + kz_s[0, x + 1, rows] * (dx + zlow(dx))
                + kz_s[1, x + 1, rows] * (y + zlow(y))
            )
            total = qx[x + 1] - qx[x] + (yhigh(qy) - qy)[rows] + (zhigh(qz) - qz)
            out.append(total * irho_s[H + x, rows])
        return jnp.stack(out)

    first_factor, factors = rkl_factors()
    inner, around = slice(H, H + cx), slice(H - 1, H + cx + 1)
    start = t_s[0, around]
    rate0 = rate(0, 1)
    r_s[...] = rate0
    t_s[1, around] = start + first_factor * rate0

    mu, nu, rest, fresh, zero = factors[0]
    second = (
        mu * t_s[1, inner, A]
        + (nu + rest) * t_s[0, inner, A]
        + zero * r_s[1 : cx + 1, A]
        + fresh * rate(1, 0)
    )
    for x in range(cx):
        for n in range(2):
            pk[0, n, x : x + 1, :] = second[x, cy - 2 + n : cy - 1 + n, :]
            pk[1, n, x : x + 1, :] = second[x, n : n + 1, :]
    t_s[2, inner, A] = second
    copies = []
    for k, (dx, dy) in enumerate(ring):
        if dy == 1:
            copies.append(remote(1, k, pk.at[0], low_row.at[dx + 1]))
        elif dy == -1:
            copies.append(remote(1, k, pk.at[1], high_row.at[dx + 1]))
        else:
            src = pl.ds(H + cx - 2 if dx == 1 else H, 2)
            dst = pl.ds(H - 2 if dx == 1 else H + cx, 2)
            copies.append(remote(1, k, t_s.at[2, src, near], t_s.at[2, dst, near]))
    mu, nu, rest, fresh, zero = factors[1]
    part = nu * t_s[1, around] + rest * t_s[0, around] + zero * r_s[...]
    for copy in copies:
        copy.wait_recv()
    sent += copies
    for x in range(-2, cx + 2):
        d = 2 if x < 0 else (0 if x >= cx else 1)
        row = x % cx
        for n in range(2):
            t_s[2, H + x, cy + n : cy + n + 1, :] = high_row[d, n, row : row + 1, :]
            t_s[2, H + x, ROWS - 2 + n : ROWS - 1 + n, :] = low_row[d, n, row : row + 1, :]
    t_s[3, around] = part + mu * t_s[2, around] + fresh * rate(2, 1)

    mu, nu, rest, fresh, zero = factors[2]
    last = (
        mu * t_s[3, inner, A]
        + nu * t_s[2, inner, A]
        + rest * t_s[0, inner, A]
        + zero * r_s[1 : cx + 1, A]
        + fresh * rate(3, 0)
    )
    o_p[...] = last * o_rho[...]
    stores.append(pltpu.make_async_copy(o_p, p_out, out_sem.at[3]))
    stores[3].start()
    for copy in sent:
        copy.wait_send()
    for store in stores:
        store.wait()


def hand_on(*refs):
    source, result, held, in_sem, out_sem = refs[:4], refs[4:8], refs[8:12], refs[12], refs[13]
    loads = [pltpu.make_async_copy(source[n], held[n], in_sem.at[n]) for n in range(4)]
    stores = [pltpu.make_async_copy(held[n], result[n], out_sem.at[n]) for n in range(4)]
    for load in loads:
        load.start()
    for load, store in zip(loads, stores):
        load.wait()
        store.start()
    for store in stores:
        store.wait()


def solution(mesh):
    nx, ny = mesh.shape["gx"], mesh.shape["gy"]

    def local(rho, v, p, b):
        cx, cy, nz = rho.shape
        wide = cx + 2 * H
        f32 = jnp.float32
        vm = lambda *shape: pltpu.VMEM(shape, f32)
        spec = pl.BlockSpec(memory_space=pl.ANY)
        shapes = [jax.ShapeDtypeStruct(a.shape, f32) for a in (rho, v, p, b)]
        results = pl.pallas_call(
            functools.partial(kernel, nx, ny),
            out_shape=shapes,
            in_specs=[pl.BlockSpec(memory_space=pltpu.HBM)] * 4,
            out_specs=[spec] * 4,
            scratch_shapes=[
                vm(cx, cy, nz),
                vm(3, cx, cy, nz),
                vm(cx, cy, nz),
                vm(3, cx, cy, nz),
                vm(8, wide, ROWS, nz),
                vm(cx, 8 * H, nz),
                vm(cx, 8 * H, nz),
                vm(wide, 8 * H, nz),
                vm(wide, 8 * H, nz),
                vm(3, wide, ROWS, nz),
                vm(7, wide, ROWS, nz),
                vm(7, wide, ROWS, nz),
                vm(7, wide, ROWS, nz),
                vm(3, ROWS, nz),
                vm(wide, ROWS, nz),
                vm(wide, ROWS, nz),
                vm(3, wide, ROWS, nz),
                vm(3, wide, ROWS, nz),
                vm(3, cx + 3, ROWS, nz),
                vm(3, cx + 3, ROWS, nz),
                vm(3, cx + 3, ROWS, nz),
                vm(SECTIONS, wide, ROWS, nz),
                vm(cx + 2, ROWS, nz),
                vm(2, 2, cx, nz),
                vm(3, 2, cx, nz),
                vm(3, 2, cx, nz),
                pltpu.SemaphoreType.DMA((2, 8)),
                pltpu.SemaphoreType.DMA((2, 8)),
                pltpu.SemaphoreType.DMA((4,)),
                pltpu.SemaphoreType.DMA((4,)),
            ],
            compiler_params=pltpu.CompilerParams(collective_id=0, has_side_effects=True),
        )(rho, v, p, b)
        return pl.pallas_call(
            hand_on,
            out_shape=shapes,
            in_specs=[spec] * 4,
            out_specs=[spec] * 4,
            scratch_shapes=[vm(*a.shape) for a in shapes]
            + [pltpu.SemaphoreType.DMA((4,)), pltpu.SemaphoreType.DMA((4,))],
        )(*results)

    placed = (
        P("gx", "gy", None),
        P(None, "gx", "gy", None),
        P("gx", "gy", None),
        P(None, "gx", "gy", None),
    )
    return jax.shard_map(
        lambda *a: tuple(local(*a)),
        mesh=mesh,
        in_specs=placed,
        out_specs=placed,
        check_vma=False,
    )
```
